128 devices in a mesh: section: 2 (over z_lo), ctx: 16 (over y, z_hi, core), tp: 4 (over x).
Axes of the slice: x: 4, y: 4, z: 4 (z_hi: 2, z_lo: 2; z = z_hi * 2 + z_lo), core: 2. Of those that a mesh axis runs over, the one named last changes fastest.
Arguments:
- frames: bfloat16 [4, 1, 1536, 768], P(None, None, 'ctx'), may hold values from -6 to 6
- w_qkv: bfloat16 [2, 768, 3, 768], P('section', 'ctx', None, 'tp'), may hold values from -0.21875 to 0.21875
- w_out: bfloat16 [2, 768, 768], P('section', 'tp', 'ctx'), may hold values from -0.21875 to 0.21875
- w_up: bfloat16 [2, 768, 3072], P('section', 'ctx', 'tp'), may hold values from -0.21875 to 0.21875
- w_down: bfloat16 [2, 3072, 768], P('section', 'tp', 'ctx'), may hold values from -0.109375 to 0.109375
- ln_gains: bfloat16 [2, 2, 768], P('section', None, 'ctx'), may hold values from 0.5 to 1.5
- shifts: bfloat16 [2, 4, 768], P('section', None, 'ctx'), may hold values from -3 to 3
- qv_bias: bfloat16 [2, 2, 768], P('section', None, ('tp', 'ctx')), may hold values from -3 to 3
- up_bias: bfloat16 [2, 3072], P('section', ('tp', 'ctx')), may hold values from -3 to 3
- lengths: int32 [4, 1], replicated, may hold values from 768 to 1536, as said below
- out_grad: bfloat16 [4, 1, 1536, 768], P(None, None, 'ctx'), may hold values from -6 to 6
Outputs:
- layer_outputs: float32 [2, 4, 1, 1536, 768], P('section', None, None, 'ctx')
- layer_input_grads: float32 [2, 4, 1, 1536, 768], P('section', None, None, 'ctx')
- grad_qkv: float32 [2, 768, 3, 768], P('section', 'ctx', None, 'tp')
- grad_out: float32 [2, 768, 768], P('section', 'tp', 'ctx')
- grad_up: float32 [2, 768, 3072], P('section', 'ctx', 'tp')
- grad_down: float32 [2, 3072, 768], P('section', 'tp', 'ctx')
- grad_gains: float32 [2, 2, 768], P('section', None, 'ctx')
- grad_shifts: float32 [2, 4, 768], P('section', None, 'ctx')
- grad_qv_bias: float32 [2, 2, 768], P('section', None, ('tp', 'ctx'))
- grad_up_bias: float32 [2, 3072], P('section', ('tp', 'ctx'))
The draws below stay inside these ranges and needn't reach their ends.
Inputs may be any that keep to these rules, and one draw needn't show every extreme that they name: `lengths`: in micro-batch 0 one clip has all 1536 frames real.
All inputs are finite; a program needn't handle non-finite values.
Results may differ from the reference program's by a relative error of at most 0.04.
Values may be sent and summed in bfloat16 or wider, within the bound.
A program may use at most 192 MiB of HBM per device.

```python
import jax
import jax.numpy as jnp
from jax import lax

D = 768
HEADS = 12
HEAD_DIM = 64
FF = 3072
SEQ = 1536
CLIPS = 1
MB = 4
LAYERS = 2


def draw_lengths(key, part):
    key = jax.random.fold_in(key, 7)
    key_base, key_pick = jax.random.split(key)
    base = jax.random.randint(key_base, (MB, CLIPS), SEQ // 2, SEQ + 1)
    chosen = jax.random.randint(key_pick, (), 0, CLIPS)
    whole = jnp.logical_and(jnp.arange(MB)[:, None] == 0, jnp.arange(CLIPS)[None, :] == chosen)
    return jnp.where(whole, SEQ, base).astype(jnp.int32)


def block_scale(own_key, shape, pieces, smallest, high):
    gain, own = 1.0, jax.random.fold_in(own_key, 6)
    for position, shards_of in pieces:
        draws = jnp.exp(jax.random.uniform(jax.random.fold_in(own, position), (shards_of,), jnp.float32, smallest / len(pieces), high / len(pieces)))
        gain = gain * jnp.repeat(draws, shape[position] // shards_of).reshape([-1 if axis == position else 1 for axis in range(len(shape))])
    return gain


def bell_draw(rng, shape, deviation, limit, cuts=(), held_as=jnp.bfloat16):
    level = block_scale(rng, shape, cuts, -0.22, 0.18) if cuts else 1.0
    values = jax.random.normal(rng, shape, jnp.float32) * deviation * level
    return jnp.minimum(jnp.maximum(values, -limit), limit).astype(held_as)


def setup_inputs(seed: int = 0) -> dict:
    key_of = jax.random.split(jax.random.key(seed), 12)
    return {
        "frames": bell_draw(key_of[0], (MB, CLIPS, SEQ, D), 1.0, 6.0, ((2, 16),)),
        "w_qkv": bell_draw(key_of[1], (LAYERS, D, 3, D), D ** -0.5, 0.21875, ((0, 2), (1, 16), (3, 4))),
        "w_out": bell_draw(key_of[2], (LAYERS, D, D), D ** -0.5, 0.21875, ((0, 2), (1, 4), (2, 16))),
        "w_up": bell_draw(key_of[3], (LAYERS, D, FF), D ** -0.5, 0.21875, ((0, 2), (1, 16), (2, 4))),
        "w_down": bell_draw(key_of[4], (LAYERS, FF, D), FF ** -0.5, 0.109375, ((0, 2), (1, 4), (2, 16))),
        "ln_gains": jnp.clip(1.0 + 0.1 * jax.random.normal(key_of[5], (LAYERS, 2, D), jnp.float32), 0.5, 1.5).astype(jnp.bfloat16),
        "shifts": bell_draw(key_of[6], (LAYERS, 4, D), 0.5, 3.0, ((0, 2), (2, 16))),
        "qv_bias": bell_draw(key_of[7], (LAYERS, 2, D), 0.5, 3.0, ((0, 2), (2, 64))),
        "up_bias": bell_draw(key_of[8], (LAYERS, FF), 0.5, 3.0, ((0, 2), (1, 64))),
        "lengths": draw_lengths(jax.random.fold_in(key_of[11], 71), 0),
        "out_grad": bell_draw(key_of[10], (MB, CLIPS, SEQ, D), 1.0, 6.0, ((2, 16),)),
    }


@jax.custom_vjp
def low(v):
    return lax.optimization_barrier(v.astype(jnp.bfloat16)).astype(jnp.float32)

@jax.custom_vjp
def low_back(v):
    return v

def low_keep(v):
    return (low(v), None)

def low_pass(kept, grad):
    return (grad,)

def back_keep(v):
    return (v, None)

def back_low(kept, grad):
    return (low(grad),)
low.defvjp(low_keep, low_pass)
low_back.defvjp(back_keep, back_low)
epsilon = 1e-05
negative = -1e+30
highest = lax.Precision.HIGHEST

def product(left, right):
    return jnp.dot(left, right, precision=highest, preferred_element_type=jnp.float32)

def normalize(values, norm_gain, norm_shift):
    center = values - lax.optimization_barrier(jnp.mean(values, axis=-1, keepdims=True))
    spread = lax.optimization_barrier(jnp.mean(center * center, axis=-1, keepdims=True))
    return center * lax.rsqrt(spread + epsilon) * norm_gain + norm_shift

def layer(layer_in, w_qkv, w_out, w_up, w_down, gain_rows, shift_rows, qv_bias, up_bias, clip_length):
    normed = low(normalize(layer_in, gain_rows[0], shift_rows[0]))
    projected = product(normed, w_qkv.reshape(D, 3 * D)).reshape(SEQ, 3, D)
    queries = low(low_back(projected[:, 0] + qv_bias[0]))
    key_rows = low(low_back(projected[:, 1]))
    value_rows = low(low_back(projected[:, 2] + qv_bias[1]))
    visible = jnp.arange(SEQ) < clip_length
    scaling = HEAD_DIM ** (-0.5)

    def one_head(per_head):
        query_head, key_head, value_head = per_head
        scores = product(query_head, key_head.T) * scaling
        scores = low_back(jnp.where(visible[None, :], scores, negative))
        shifted = scores - lax.optimization_barrier(jnp.max(scores, axis=-1, keepdims=True))
        raised = jnp.exp(shifted)
        softmax_w = raised / lax.optimization_barrier(jnp.sum(raised, axis=-1, keepdims=True))
        return product(low(softmax_w), value_head)

    def by_heads(array):
        return array.reshape(SEQ, HEADS, HEAD_DIM).transpose(1, 0, 2)
    head_out = lax.map(jax.checkpoint(one_head), (by_heads(queries), by_heads(key_rows), by_heads(value_rows)))
    attended = low(low_back(head_out.transpose(1, 0, 2).reshape(SEQ, D)))
    attn_out = low_back(product(attended, w_out) + shift_rows[2])
    middle = layer_in + attn_out
    normed2 = low(normalize(middle, gain_rows[1], shift_rows[1]))
    hidden_pre = low_back(product(normed2, w_up) + up_bias)
    activated = low(jax.nn.gelu(hidden_pre, approximate=False))
    down_out = low_back(product(activated, w_down) + shift_rows[3])
    return middle + down_out

def reference(frames, w_qkv, w_out, w_up, w_down, ln_gains, shifts, qv_bias, up_bias, lengths, out_grad):
    params = [param.astype(jnp.float32) for param in (w_qkv, w_out, w_up, w_down, ln_gains, shifts, qv_bias, up_bias)]
    layer_zero = tuple((param[0] for param in params))
    second = tuple((param[1] for param in params))
    inputs = frames.astype(jnp.float32).reshape(MB * CLIPS, SEQ, D)
    cotangents = out_grad.astype(jnp.float32).reshape(MB * CLIPS, SEQ, D)
    clip_lengths = lengths.reshape(MB * CLIPS)

    def clip_step(summed_grads, per_clip):
        layer_val, clip_length, cotangent = per_clip

        def apply_layer(values, *weights):
            return layer(values, *weights, clip_length)
        out_zero, back_zero = jax.vjp(apply_layer, layer_val, *layer_zero)
        hidden = low(out_zero)
        out_one, back_one = jax.vjp(apply_layer, hidden, *second)
        grads_one = back_one(cotangent)
        grads_zero = back_zero(low(grads_one[0]))
        summed_grads = tuple((running + jnp.stack([left_grad, right_grad]) for running, left_grad, right_grad in zip(summed_grads, grads_zero[1:], grads_one[1:])))
        return (summed_grads, (out_zero, out_one, grads_zero[0], grads_one[0]))
    zeros = tuple((jnp.zeros_like(param) for param in params))
    summed_grads, (first_out, final_out, input_grad, hidden_grad) = lax.scan(clip_step, zeros, (inputs, clip_lengths, cotangents))
    full_shape = (MB, CLIPS, SEQ, D)
    layer_outputs = jnp.stack([first_out.reshape(full_shape), final_out.reshape(full_shape)])
    layer_input_grads = jnp.stack([input_grad.reshape(full_shape), hidden_grad.reshape(full_shape)])
    return (layer_outputs, layer_input_grads, summed_grads[0], summed_grads[1], summed_grads[2], summed_grads[3], summed_grads[4], summed_grads[5], summed_grads[6], summed_grads[7])
```

```python
import functools

import jax
import jax.numpy as jnp
import numpy as np
from jax import lax
from jax.experimental import pallas as pl
from jax.experimental.pallas import tpu as pltpu
from jax.sharding import PartitionSpec as P

MESH = pl.DeviceIdType.MESH
f32 = jnp.float32
bf16 = jnp.bfloat16
epsilon = 1e-05
negative = -1e30

D = 768
SHARD = 48
QUARTER = 48
BLOCK = 96
ROWS = 192
KEYS = 1536
Q0, KV0, OUT0, UP0, DOWN0, WIDE = 0, 256, 640, 896, 1664, 2432
HALF = 1280
PIECE = 256
HEADS3 = 3
VMEM_LIMIT = 60 * 1024 * 1024


def where_am_i():
    s = lax.axis_index("section")
    c = lax.axis_index("ctx")
    t = lax.axis_index("tp")
    y = lax.div(c, 4)
    zh = lax.rem(lax.div(c, 2), 2)
    core = lax.rem(c, 2)
    return y, zh * 2 + s, core, t


def ident(y, z, core, t):
    return {"section": lax.rem(z, 2), "ctx": y * 4 + lax.div(z, 2) * 2 + core, "tp": t}


def ring(i, d):
    return lax.rem(i + d, 4)


def greet(peers):
    barrier = pltpu.get_barrier_semaphore()
    for peer in peers:
        pl.semaphore_signal(barrier, inc=1, device_id=peer, device_id_type=MESH)
    pl.semaphore_wait(barrier, len(peers))


def remote(src, dst, send, recv, peer):
    return pltpu.make_async_remote_copy(
        src_ref=src, dst_ref=dst, send_sem=send, recv_sem=recv, device_id=peer, device_id_type=MESH
    )


def gather_kernel(w_ref, f_ref, g_ref, w_all, x_all, g_all, send, recv, local):
    y, z, core, t = where_am_i()
    other = 1 - core

    def spot(da, db):
        return ring(y, da * core + db * other), ring(z, da * other + db * core)

    def peer(da, db):
        yy, zz = spot(da, db)
        return ident(yy, zz, core, t)

    def block(da, db, of_core, half=None):
        yy, zz = spot(da, db)
        row = pl.multiple_of((yy * 4 + lax.div(zz, 2) * 2 + of_core) * SHARD, SHARD)
        cols = {None: pl.ds(0, WIDE), 0: pl.ds(0, HALF), 1: pl.ds(HALF, WIDE - HALF)}[half]
        return w_all.at[lax.rem(zz, 2), pl.ds(row, SHARD), cols]

    zh = lax.div(z, 2)
    twin = ident(y, 3 - z, core, t)
    mate = ident(y, z, other, t)
    greet([peer(1, 0), peer(3, 0), peer(0, 1), peer(0, 3), mate])

    sent = []

    def put(k, src, dst, to):
        copy = remote(src, dst, send.at[k], recv.at[k], to)
        copy.start()
        sent.append(copy)

    def got(k, region):
        remote(region, region, send.at[k], recv.at[k], mate).wait_recv()

    own = block(0, 0, core)
    put(0, w_ref, own, peer(1, 0))
    put(1, w_ref, own, peer(3, 0))
    put(4, w_ref, own, peer(0, 1))
    put(5, w_ref, own, peer(0, 3))
    put(20, w_ref, own, mate)
    mine = pl.ds(pl.multiple_of(zh * BLOCK, BLOCK), BLOCK)
    theirs = pl.ds(pl.multiple_of((1 - zh) * BLOCK, BLOCK), BLOCK)
    put(36, f_ref.at[3 - z], x_all.at[mine], twin)
    put(37, g_ref.at[3 - z], g_all.at[mine], twin)
    kept = [
        pltpu.make_async_copy(w_ref, own, local.at[0]),
        pltpu.make_async_copy(f_ref.at[z], x_all.at[mine], local.at[1]),
        pltpu.make_async_copy(g_ref.at[z], g_all.at[mine], local.at[2]),
    ]
    for copy in kept:
        copy.start()

    def spread(j, da):
        put(4 + 4 * j, block(da, 0, core), block(da, 0, core), peer(0, 1))
        put(5 + 4 * j, block(da, 0, core), block(da, 0, core), peer(0, 3))
        put(20 + 4 * j, block(da, 0, core), block(da, 0, core), mate)

    got(0, block(3, 0, core))
    put(2, block(3, 0, core, 0), block(3, 0, core, 0), peer(1, 0))
    spread(1, 3)
    got(1, block(1, 0, core))
    put(3, block(1, 0, core, 1), block(1, 0, core, 1), peer(3, 0))
    spread(2, 1)

    def second(j, da):
        k = 4 + 4 * j
        got(k, block(da, 3, core))
        put(k + 2, block(da, 3, core, 0), block(da, 3, core, 0), peer(0, 1))
        put(20 + 4 * j + 1, block(da, 3, core), block(da, 3, core), mate)
        got(k + 1, block(da, 1, core))
        put(k + 3, block(da, 1, core, 1), block(da, 1, core, 1), peer(0, 3))
        put(20 + 4 * j + 2, block(da, 1, core), block(da, 1, core), mate)

    def last(j, da):
        k = 4 + 4 * j
        got(k + 2, block(da, 2, core, 0))
        got(k + 3, block(da, 2, core, 1))
        put(20 + 4 * j + 3, block(da, 2, core), block(da, 2, core), mate)

    second(0, 0)
    got(2, block(2, 0, core, 0))
    got(3, block(2, 0, core, 1))
    spread(3, 2)
    second(1, 3)
    last(0, 0)
    second(2, 1)
    last(1, 3)
    second(3, 2)
    last(2, 1)
    last(3, 2)
    for k in range(16):
        got(20 + k, own)
    got(36, x_all.at[theirs])
    got(37, g_all.at[theirs])
    for copy in kept:
        copy.wait()
    for copy in sent:
        copy.wait_send()


def gather_call(w, frames, out_grad):
    anywhere = pl.BlockSpec(memory_space=pl.ANY)
    return pl.pallas_call(
        gather_kernel,
        out_shape=(
            jax.ShapeDtypeStruct((2, D, WIDE), bf16),
            jax.ShapeDtypeStruct((ROWS, D), bf16),
            jax.ShapeDtypeStruct((ROWS, D), bf16),
        ),
        in_specs=[anywhere] * 3,
        out_specs=(anywhere,) * 3,
        scratch_shapes=[
            pltpu.SemaphoreType.DMA((38,)),
            pltpu.SemaphoreType.DMA((38,)),
            pltpu.SemaphoreType.DMA((3,)),
        ],
        compiler_params=pltpu.CompilerParams(collective_id=0, has_side_effects=True),
        name="weights_to_all",
    )(w, frames, out_grad)


def dot(a, b):
    return lax.dot_general(a, b, (((1,), (0,)), ((), ())), preferred_element_type=f32)


def dot_t(a, b):
    return lax.dot_general(a, b, (((1,), (1,)), ((), ())), preferred_element_type=f32)


def hat(v):
    center = v - jnp.mean(v, axis=-1, keepdims=True)
    r = lax.rsqrt(jnp.mean(center * center, axis=-1, keepdims=True) + epsilon)
    return center * r, r


def norm(v, gain, shift):
    return hat(v)[0] * gain + shift


def norm_back(v, gain, c):
    vhat, r = hat(v)
    cg = c * gain
    grad = r * (
        cg - jnp.mean(cg, axis=-1, keepdims=True) - vhat * jnp.mean(cg * vhat, axis=-1, keepdims=True)
    )
    return grad, jnp.sum(c * vhat, axis=0, keepdims=True), jnp.sum(c, axis=0, keepdims=True)


def layers_kernel(
    w_hbm, x_ref, g_ref, keep_ref, sel_ref,
    kept_ref, grads_ref,
    w_ref, w_sem, n1, n2, gdi0, ga, rs, part, kv, att, act, slope, mid, lse, q, small, scores, acc,
    dkv, dqkv, core_in, step_out, step1, step2, little,
    x_send, x_recv, k_send, k_recv,
):
    y, z, core, t = where_am_i()
    other = 1 - core
    mate = ident(y, z, other, t)
    up_peer = ident(ring(y, 1), z, core, t)
    down_peer = ident(ring(y, 3), z, core, t)
    loads = [pltpu.make_async_copy(w_hbm.at[l], w_ref.at[l], w_sem.at[l]) for l in range(2)]
    for load in loads:
        load.start()
    greet([ident(y, z, core, ring(t, d)) for d in (1, 2, 3)] + [up_peer, down_peer, mate])
    sent = []
    quarter = pl.ds(pl.multiple_of(t * QUARTER, QUARTER), QUARTER)

    def put(src, dst, send, recv, to):
        copy = remote(src, dst, send, recv, to)
        copy.start()
        sent.append(copy)

    def got(region, send, recv):
        remote(region, region, send, recv, mate).wait_recv()

    def rows_of(i):
        return pl.ds(pl.multiple_of(i * QUARTER, QUARTER), QUARTER)

    def share_start(phase, ref):
        for d in (1, 2, 3):
            put(ref.at[quarter], ref.at[quarter], x_send.at[phase, d - 1], x_recv.at[phase, d - 1],
                ident(y, z, core, ring(t, d)))

    def share_wait(phase, ref):
        for d in (1, 2, 3):
            got(ref.at[rows_of(ring(t, 4 - d))], x_send.at[phase, d - 1], x_recv.at[phase, d - 1])

    def sum_start(phase, i):
        for d in (1, 2, 3):
            put(part.at[i, rows_of(ring(t, d))], rs.at[i, d - 1], x_send.at[phase, d - 1],
                x_recv.at[phase, d - 1], ident(y, z, core, ring(t, d)))

    def sum_wait(phase, i):
        total = part[i, quarter, :].astype(f32)
        for d in (1, 2, 3):
            got(rs.at[i, d - 1], x_send.at[phase, d - 1], x_recv.at[phase, d - 1])
            total = total + rs[i, d - 1].astype(f32)
        return total

    col = lax.broadcasted_iota(jnp.int32, (1, 256), 1)
    q_masks = [jnp.where((col >= 64 * h) & (col < 64 * h + 64), 1.0, 0.0).astype(f32) for h in range(3)]
    v_masks = [jnp.where((col >= 64 * h + 64) & (col < 64 * h + 128), 1.0, 0.0).astype(f32) for h in range(3)]

    def by_head(rows, masks):
        rows = rows.astype(f32)
        return jnp.concatenate([rows * m for m in masks], axis=0)

    def from_heads(rows, masks):
        return sum(rows[h * ROWS : (h + 1) * ROWS] * masks[h] for h in range(3))

    def kv_rows(yy, of_core, first=0, size=ROWS):
        return pl.ds(pl.multiple_of((yy * 2 + of_core) * ROWS + first, BLOCK), size)

    def load_small(l):
        loads[l].wait()
        tile = w_ref[l, :, OUT0 : OUT0 + 128].astype(f32).T
        small[l] = tile[:16]

    def kv_share(l):
        buf = kv.at[l]
        s, r = k_send.at[l], k_recv.at[l]
        own = buf.at[kv_rows(y, core)]
        put(own, own, s.at[0], r.at[0], up_peer)
        put(own, own, s.at[1], r.at[1], down_peer)
        put(own, own, s.at[4], r.at[4], mate)
        before, after, across = ring(y, 3), ring(y, 1), ring(y, 2)
        whole = buf.at[kv_rows(before, core)]
        got(whole, s.at[0], r.at[0])
        first = buf.at[kv_rows(before, core, 0, BLOCK)]
        put(first, first, s.at[2], r.at[2], up_peer)
        put(whole, whole, s.at[5], r.at[5], mate)
        whole = buf.at[kv_rows(after, core)]
        got(whole, s.at[1], r.at[1])
        second = buf.at[kv_rows(after, core, BLOCK, BLOCK)]
        put(second, second, s.at[3], r.at[3], down_peer)
        put(whole, whole, s.at[6], r.at[6], mate)
        for i, k in ((0, 2), (1, 3)):
            piece = buf.at[kv_rows(across, core, i * BLOCK, BLOCK)]
            got(piece, s.at[k], r.at[k])
            put(piece, piece, s.at[7 + i], r.at[7 + i], mate)
        got(buf.at[kv_rows(y, other)], s.at[4], r.at[4])
        got(buf.at[kv_rows(before, other)], s.at[5], r.at[5])
        got(buf.at[kv_rows(after, other)], s.at[6], r.at[6])
        got(buf.at[kv_rows(across, other, 0, BLOCK)], s.at[7], r.at[7])
        got(buf.at[kv_rows(across, other, BLOCK, BLOCK)], s.at[8], r.at[8])

    def attend(l):
        q3 = by_head(q[l], q_masks).astype(bf16)

        def first(i, top):
            at = pl.ds(pl.multiple_of(i * PIECE, PIECE), PIECE)
            s = dot_t(kv[l, at, 0:256], q3)
            s = jnp.where(keep_ref[at, :] < 0, negative, s)
            scores[at, :] = s
            return jnp.maximum(top, jnp.max(s, axis=0, keepdims=True))

        top = lax.fori_loop(0, KEYS // PIECE, first, jnp.full((1, 3 * ROWS), negative, f32))
        acc[...] = jnp.zeros_like(acc)

        def second(i, total):
            at = pl.ds(pl.multiple_of(i * PIECE, PIECE), PIECE)
            p = jnp.exp(scores[at, :] - top)
            acc[...] += dot(kv[l, at, 128:384].T, p.astype(bf16))
            return total + jnp.sum(p, axis=0, keepdims=True)

        total = lax.fori_loop(0, KEYS // PIECE, second, jnp.zeros((1, 3 * ROWS), f32))
        lse[l] = top + jnp.log(total)
        att[l] = from_heads((acc[...] / total).T, v_masks).astype(bf16)

    def forward(l, x_q):
        row = small[l]
        bias = dot(row.astype(bf16), sel_ref[...])
        wide = dot(n1[l], w_ref[l, :, Q0:OUT0])
        q[l] = ((wide[:, :256] + bias[7:8, :256]).astype(bf16).astype(f32) * 0.125).astype(bf16)
        kv[l, kv_rows(y, core), :] = (wide[:, 256:] + bias[8:9, 256:]).astype(bf16)
        kv_share(l)
        attend(l)
        part[2 * l] = dot_t(att[l], w_ref[l, :, OUT0:UP0]).astype(bf16)
        sum_start(4 * l, 2 * l)
        m = x_q + sum_wait(4 * l, 2 * l) + row[4:5]
        mid[l] = m
        n2[l, quarter, :] = norm(m, row[1:2], row[3:4]).astype(bf16)
        share_start(4 * l + 1, n2.at[l])
        share_wait(4 * l + 1, n2.at[l])
        u = dot(n2[l], w_ref[l, :, UP0:DOWN0]) + row[6:7]
        phi = 0.5 * (1.0 + lax.erf(u * np.float32(0.5**0.5)))
        act[l] = (u * phi).astype(bf16)
        part[2 * l + 1] = dot_t(act[l], w_ref[l, :, DOWN0:WIDE]).astype(bf16)
        sum_start(4 * l + 2, 2 * l + 1)
        slope[l] = phi + u * jnp.exp(-0.5 * u * u) * np.float32((2 * np.pi) ** -0.5)
        out = m + sum_wait(4 * l + 2, 2 * l + 1) + row[5:6]
        kept_ref[l, 0] = out.astype(bf16)
        return out

    def dkv_sum(l):
        s, r = k_send.at[2 + l], k_recv.at[2 + l]
        for i in range(4):
            put(dkv.at[l, kv_rows(i, other)], core_in.at[l, i], s.at[i], r.at[i], mate)

        def mine(yy):
            return dkv[l, kv_rows(yy, core), :].astype(f32) + core_in[l, yy].astype(f32)

        for i in range(4):
            got(core_in.at[l, i], s.at[i], r.at[i])
        before, after, across = ring(y, 3), ring(y, 1), ring(y, 2)
        step_out[l, 0] = mine(across).astype(bf16)
        put(step_out.at[l, 0, pl.ds(0, BLOCK)], step1.at[l, 0], s.at[4], r.at[4], up_peer)
        put(step_out.at[l, 0, pl.ds(BLOCK, BLOCK)], step1.at[l, 1], s.at[5], r.at[5], down_peer)
        to_up, to_down, here = mine(after), mine(before), mine(y)
        got(step1.at[l, 0], s.at[4], r.at[4])
        step_out[l, 1, :BLOCK, :] = (to_up[:BLOCK] + step1[l, 0].astype(f32)).astype(bf16)
        step_out[l, 1, BLOCK:, :] = to_up[BLOCK:].astype(bf16)
        put(step_out.at[l, 1], step2.at[l, 0], s.at[6], r.at[6], up_peer)
        got(step1.at[l, 1], s.at[5], r.at[5])
        step_out[l, 2, :BLOCK, :] = to_down[:BLOCK].astype(bf16)
        step_out[l, 2, BLOCK:, :] = (to_down[BLOCK:] + step1[l, 1].astype(f32)).astype(bf16)
        put(step_out.at[l, 2], step2.at[l, 1], s.at[7], r.at[7], down_peer)
        got(step2.at[l, 0], s.at[6], r.at[6])
        got(step2.at[l, 1], s.at[7], r.at[7])
        return here + step2[l, 0].astype(f32) + step2[l, 1].astype(f32)

    def attend_back(l, grad_att):
        q3 = by_head(q[l], q_masks).astype(bf16)
        do3 = by_head(grad_att, v_masks)
        o3 = by_head(att[l], v_masks)
        delta = jnp.sum((do3 * o3).T, axis=0, keepdims=True)
        do3 = do3.astype(bf16)
        acc[...] = jnp.zeros_like(acc)
        log_total = lse[l]

        def step(i, carry):
            at = pl.ds(pl.multiple_of(i * PIECE, PIECE), PIECE)
            k = kv[l, at, 0:256]
            s = jnp.where(keep_ref[at, :] < 0, negative, dot_t(k, q3))
            p = jnp.exp(s - log_total)
            ds = (p * (dot_t(kv[l, at, 128:384], do3) - delta)).astype(bf16)
            dk = dot(ds, q3)
            dv = dot(p.astype(bf16), do3)
            dkv[l, at, 0:128] = dk[:, :128].astype(bf16)
            dkv[l, at, 128:256] = (dk[:, 128:] + dv[:, :128]).astype(bf16)
            dkv[l, at, 256:384] = dv[:, 128:].astype(bf16)
            acc[...] += dot(k.T, ds)
            return carry

        lax.fori_loop(0, KEYS // PIECE, step, 0)
        dqkv[l, :, 0:256] = (from_heads(acc[...].T, q_masks) * 0.125).astype(bf16)

    def backward(l, dout_q, gdi_ref, x_q):
        base = 8 + 4 * (1 - l)
        row = small[l]
        gdi = gdi_ref[...]
        gpre = (dot(gdi, w_ref[l, :, DOWN0:WIDE]) * slope[l]).astype(bf16)
        part[4 + 2 * l] = dot_t(gpre, w_ref[l, :, UP0:DOWN0]).astype(bf16)
        sum_start(base, 4 + 2 * l)
        grads_ref[l, :, UP0:DOWN0] = dot(n2[l].T, gpre).astype(bf16)
        grads_ref[l, :, DOWN0:WIDE] = dot(gdi.T, act[l]).astype(bf16)
        little[l] = jnp.zeros_like(little[l])
        little[l, 6:7, :] = jnp.sum(gpre.astype(f32), axis=0, keepdims=True)
        little[l, 5:6, :] = jnp.sum(dout_q, axis=0, keepdims=True)
        c = sum_wait(base, 4 + 2 * l)
        gv, g_gain, g_shift = norm_back(mid[l], row[1:2], c)
        gm = dout_q + gv
        low = gm.astype(bf16)
        ga[l, quarter, :] = low
        share_start(base + 1, ga.at[l])
        little[l, 1:2, :] = g_gain
        little[l, 3:4, :] = g_shift
        little[l, 4:5, :] = jnp.sum(low.astype(f32), axis=0, keepdims=True)
        share_wait(base + 1, ga.at[l])
        grad_att = dot(ga[l], w_ref[l, :, OUT0:UP0]).astype(bf16)
        attend_back(l, grad_att)
        dqkv[l, :, 256:640] = dkv_sum(l).astype(bf16)
        part[5 + 2 * l] = dot_t(dqkv[l], w_ref[l, :, Q0:OUT0]).astype(bf16)
        sum_start(base + 2, 5 + 2 * l)
        grads_ref[l, :, Q0:OUT0] = dot(n1[l].T, dqkv[l]).astype(bf16)
        sums = jnp.sum(dqkv[l].astype(f32), axis=0, keepdims=True)
        wide_col = lax.broadcasted_iota(jnp.int32, (8, 640), 1)
        which = lax.broadcasted_iota(jnp.int32, (8, 640), 0)
        two = jnp.where(((wide_col < 256) & (which == 0)) | ((wide_col >= 256) & (which == 1)), sums, 0.0)
        placed = dot_t(two.astype(bf16), sel_ref[...])
        little[l, 7:9, :] = placed[0:2]
        c = sum_wait(base + 2, 5 + 2 * l)
        gv, g_gain, g_shift = norm_back(x_q, row[0:1], c)
        little[l, 0:1, :] = g_gain
        little[l, 2:3, :] = g_shift
        gx = gm + gv
        kept_ref[l, 1] = gx.astype(bf16)
        return gx

    def out_grads(l):
        both = dot(ga[l].T, att[l])
        grads_ref[l, :, OUT0 : OUT0 + 128] = (both[:, :128] + little[l].T).astype(bf16)
        grads_ref[l, :, OUT0 + 128 : UP0] = both[:, 128:].astype(bf16)

    load_small(0)
    n1[0] = norm(x_ref[...].astype(f32), small[0, 0:1, :], small[0, 2:3, :]).astype(bf16)
    x0 = x_ref[quarter, :].astype(f32)
    x1 = forward(0, x0).astype(bf16).astype(f32)
    load_small(1)
    n1[1, quarter, :] = norm(x1, small[1, 0:1, :], small[1, 2:3, :]).astype(bf16)
    share_start(3, n1.at[1])
    share_wait(3, n1.at[1])
    forward(1, x1)
    gx = backward(1, g_ref[quarter, :].astype(f32), g_ref, x1).astype(bf16)
    gdi0[quarter, :] = gx
    share_start(11, gdi0)
    out_grads(1)
    share_wait(11, gdi0)
    backward(0, gx.astype(f32), gdi0, x0)
    out_grads(0)
    for copy in sent:
        copy.wait_send()


def layers_call(w, x, g, keep, sel):
    vmem = pl.BlockSpec(memory_space=pltpu.VMEM)
    return pl.pallas_call(
        layers_kernel,
        out_shape=(
            jax.ShapeDtypeStruct((2, 2, QUARTER, D), bf16),
            jax.ShapeDtypeStruct((2, D, WIDE), bf16),
        ),
        in_specs=[pl.BlockSpec(memory_space=pl.ANY)] + [vmem] * 4,
        out_specs=(vmem, vmem),
        scratch_shapes=[
            pltpu.VMEM((2, D, WIDE), bf16),
            pltpu.SemaphoreType.DMA((2,)),
            pltpu.VMEM((2, ROWS, D), bf16),
            pltpu.VMEM((2, ROWS, D), bf16),
            pltpu.VMEM((ROWS, D), bf16),
            pltpu.VMEM((2, ROWS, D), bf16),
            pltpu.VMEM((8, 3, QUARTER, D), bf16),
            pltpu.VMEM((8, ROWS, D), bf16),
            pltpu.VMEM((2, KEYS, 384), bf16),
            pltpu.VMEM((2, ROWS, 256), bf16),
            pltpu.VMEM((2, ROWS, D), bf16),
            pltpu.VMEM((2, ROWS, D), f32),
            pltpu.VMEM((2, QUARTER, D), f32),
            pltpu.VMEM((2, 1, 3 * ROWS), f32),
            pltpu.VMEM((2, ROWS, 256), bf16),
            pltpu.VMEM((2, 16, D), f32),
            pltpu.VMEM((KEYS, 3 * ROWS), f32),
            pltpu.VMEM((256, 3 * ROWS), f32),
            pltpu.VMEM((2, KEYS, 384), bf16),
            pltpu.VMEM((2, ROWS, 640), bf16),
            pltpu.VMEM((2, 4, ROWS, 384), bf16),
            pltpu.VMEM((2, 3, ROWS, 384), bf16),
            pltpu.VMEM((2, 2, BLOCK, 384), bf16),
            pltpu.VMEM((2, 2, ROWS, 384), bf16),
            pltpu.VMEM((2, 128, D), f32),
            pltpu.SemaphoreType.DMA((16, 3)),
            pltpu.SemaphoreType.DMA((16, 3)),
            pltpu.SemaphoreType.DMA((4, 9)),
            pltpu.SemaphoreType.DMA((4, 9)),
        ],
        compiler_params=pltpu.CompilerParams(
            collective_id=1, has_side_effects=True, vmem_limit_bytes=VMEM_LIMIT
        ),
        name="layers",
    )(w, x, g, keep, sel)


def scatter_kernel(
    g_ref, kept_ref, own_ref, tile_ref, dist_ref,
    core_in, halves0, halves1, fulls, out1, out2, tiles, send, recv, d_send, d_recv, t_send, t_recv, d_local,
):
    y, z, core, t = where_am_i()
    other = 1 - core
    zh = lax.div(z, 2)
    h = lax.div(t, 2)

    def spot(da, db):
        return ring(y, da * core + db * other), ring(z, da * other + db * core)

    def peer(da, db):
        yy, zz = spot(da, db)
        return ident(yy, zz, core, t)

    def rows_at(yy, zz, of_core):
        return pl.ds(pl.multiple_of((yy * 4 + lax.div(zz, 2) * 2 + of_core) * SHARD, SHARD), SHARD)

    mate = ident(y, z, other, t)
    plane = [ident(y, ring(z, a), core, ring(t, b)) for a in range(4) for b in range(4) if a or b]
    greet(plane + [ident(ring(y, 1), z, core, t), ident(ring(y, 3), z, core, t), mate])
    sent = []

    def put(src, dst, s, r, to):
        copy = remote(src, dst, s, r, to)
        copy.start()
        sent.append(copy)

    def got(region, s, r):
        remote(region, region, s, r, mate).wait_recv()

    for yy in range(4):
        for zz in range(4):
            k = 20 + yy * 4 + zz
            put(g_ref.at[zz % 2, rows_at(yy, zz, other)], core_in.at[yy * 4 + zz], send.at[k], recv.at[k], mate)

    for l in range(2):
        for a in range(4):
            to_z = h * 2 + l
            here = jnp.logical_and(to_z == z, t == a)
            dst = dist_ref.at[z, lax.rem(t, 2)]

            @pl.when(here)
            def _():
                pltpu.make_async_copy(kept_ref.at[l], dst, d_local).start()

            @pl.when(jnp.logical_not(here))
            def _():
                remote(kept_ref.at[l], dst, d_send.at[l, a], d_recv.at[z, lax.rem(t, 2)],
                       ident(y, to_z, core, a)).start()

    def mine(da, db):
        yy, zz = spot(da, db)
        return g_ref[lax.rem(zz, 2), rows_at(yy, zz, core), :].astype(f32) + core_in[yy * 4 + zz].astype(f32)

    for k in range(16):
        got(core_in.at[k], send.at[20 + k], recv.at[20 + k])

    def first(j, far, to):
        out1[j] = far.astype(bf16)
        k = 4 * j
        put(out1.at[j, :, pl.ds(0, HALF)], halves0.at[j], send.at[k], recv.at[k], to[0])
        put(out1.at[j, :, pl.ds(HALF, WIDE - HALF)], halves1.at[j], send.at[k + 1], recv.at[k + 1], to[1])

    def second(j, ahead, behind, to):
        k = 4 * j
        got(halves0.at[j], send.at[k], recv.at[k])
        out2[j, 0, :, :HALF] = (ahead[:, :HALF] + halves0[j].astype(f32)).astype(bf16)
        out2[j, 0, :, HALF:] = ahead[:, HALF:].astype(bf16)
        put(out2.at[j, 0], fulls.at[j, 0], send.at[k + 2], recv.at[k + 2], to[0])
        got(halves1.at[j], send.at[k + 1], recv.at[k + 1])
        out2[j, 1, :, :HALF] = behind[:, :HALF].astype(bf16)
        out2[j, 1, :, HALF:] = (behind[:, HALF:] + halves1[j].astype(f32)).astype(bf16)
        put(out2.at[j, 1], fulls.at[j, 1], send.at[k + 3], recv.at[k + 3], to[1])

    def third(j, own):
        k = 4 * j
        got(fulls.at[j, 0], send.at[k + 2], recv.at[k + 2])
        got(fulls.at[j, 1], send.at[k + 3], recv.at[k + 3])
        return own + fulls[j, 0].astype(f32) + fulls[j, 1].astype(f32)

    ring_b = (peer(0, 1), peer(0, 3))
    ring_a = (peer(1, 0), peer(3, 0))
    order = (2, 1, 3, 0)
    for da in order:
        first(da, mine(da, 2), ring_b)
    for da in order:
        second(da, mine(da, 1), mine(da, 3), ring_b)
    first(4, third(2, mine(2, 0)), ring_a)
    second(4, third(1, mine(1, 0)), third(3, mine(3, 0)), ring_a)
    total = third(4, third(0, mine(0, 0)))
    own_ref[...] = total
    tiles[0] = total[:, OUT0 : OUT0 + 128]
    for d in (1, 2, 3):
        put(tiles.at[0], tiles.at[d], t_send.at[d - 1], t_recv.at[d - 1], ident(y, z, core, ring(t, d)))
    tile = tiles[0]
    for d in (1, 2, 3):
        got(tiles.at[d], t_send.at[d - 1], t_recv.at[d - 1])
        tile = tile + tiles[d]
    tile_ref[...] = tile

    for l in range(2):
        for a in range(4):
            to_z = h * 2 + l
            here = jnp.logical_and(to_z == z, t == a)
            dst = dist_ref.at[z, lax.rem(t, 2)]

            @pl.when(here)
            def _():
                pltpu.make_async_copy(kept_ref.at[l], dst, d_local).wait()

            @pl.when(jnp.logical_not(here))
            def _():
                remote(kept_ref.at[l], dst, d_send.at[l, a], d_recv.at[z, lax.rem(t, 2)],
                       ident(y, to_z, core, a)).wait_send()

    for zz in range(4):
        for b in range(2):
            from_here = jnp.logical_and(zz == z, t == zh * 2 + b)

            @pl.when(jnp.logical_not(from_here))
            def _():
                got(dist_ref.at[zz, b], d_send.at[0, 0], d_recv.at[zz, b])

    for copy in sent:
        copy.wait_send()


def scatter_call(grads, kept):
    vmem = pl.BlockSpec(memory_space=pltpu.VMEM)
    return pl.pallas_call(
        scatter_kernel,
        out_shape=(
            jax.ShapeDtypeStruct((SHARD, WIDE), f32),
            jax.ShapeDtypeStruct((SHARD, 128), f32),
            jax.ShapeDtypeStruct((4, 2, 2, QUARTER, D), bf16),
        ),
        in_specs=[vmem] * 2,
        out_specs=(vmem,) * 3,
        scratch_shapes=[
            pltpu.VMEM((16, SHARD, WIDE), bf16),
            pltpu.VMEM((5, SHARD, HALF), bf16),
            pltpu.VMEM((5, SHARD, WIDE - HALF), bf16),
            pltpu.VMEM((5, 2, SHARD, WIDE), bf16),
            pltpu.VMEM((5, SHARD, WIDE), bf16),
            pltpu.VMEM((5, 2, SHARD, WIDE), bf16),
            pltpu.VMEM((4, SHARD, 128), f32),
            pltpu.SemaphoreType.DMA((36,)),
            pltpu.SemaphoreType.DMA((36,)),
            pltpu.SemaphoreType.DMA((2, 4)),
            pltpu.SemaphoreType.DMA((4, 2)),
            pltpu.SemaphoreType.DMA((3,)),
            pltpu.SemaphoreType.DMA((3,)),
            pltpu.SemaphoreType.DMA,
        ],
        compiler_params=pltpu.CompilerParams(
            collective_id=2, has_side_effects=True, vmem_limit_bytes=VMEM_LIMIT
        ),
        name="gradients_to_owners",
    )(grads, kept)


def selection():
    sel = np.zeros((D, 640), np.float32)
    for c in range(16):
        for i in range(12):
            sel[c * 48 + i, c * 12 + i] = 1.0
            sel[c * 48 + i, 448 + c * 12 + i] = 1.0
    return sel


def key_frames():
    r = np.arange(KEYS)
    j, w = r // ROWS, r % ROWS
    y, core = j // 2, j % 2
    hi = w // BLOCK
    return (((y * 2 + hi) * 2 + core) * BLOCK + w % BLOCK).astype(np.int32)


def on_device(
    frames, w_qkv, w_out, w_up, w_down, ln_gains, shifts, qv_bias, up_bias, lengths, out_grad
):
    _, z, _, _ = where_am_i()
    pad = ((0, 0), (0, SHARD - 12))
    little = jnp.concatenate(
        [ln_gains[0], shifts[0], up_bias, jnp.pad(qv_bias[0], pad), jnp.zeros((55, SHARD), bf16)], axis=0
    )
    packed = jnp.concatenate(
        [
            w_qkv[0, :, 0], jnp.zeros((SHARD, 64), bf16), w_qkv[0, :, 1], w_qkv[0, :, 2],
            little.T, w_out[0].T, w_up[0], w_down[0].T,
        ],
        axis=1,
    )
    w_all, x, g = gather_call(packed, frames[:, 0], out_grad[:, 0])
    length = lax.dynamic_index_in_dim(lengths, z, 0, keepdims=False)[0]
    keep = jnp.where(jnp.asarray(key_frames())[:, None] < length, 0.0, -1.0).astype(f32)
    kept, grads = layers_call(w_all, x, g, keep, jnp.asarray(selection(), bf16))
    own, tile, dist = scatter_call(grads, kept)
    outs = dist.astype(f32)
    tile_t = tile.T
    little_t = own[:, OUT0 : OUT0 + 64].T
    grad_qkv = jnp.stack([own[:, 0:192], own[:, 256:448], own[:, 448:640]], axis=1)
    return (
        outs[:, :, 0].reshape(1, 4, 1, BLOCK, D),
        outs[:, :, 1].reshape(1, 4, 1, BLOCK, D),
        grad_qkv[None],
        own[:, OUT0 + 64 : UP0].T[None],
        own[:, UP0:DOWN0][None],
        own[:, DOWN0:WIDE].T[None],
        tile_t[0:2][None],
        tile_t[2:6][None],
        little_t[7:9, :12][None],
        little_t[6:7],
    )


def solution(mesh):
    in_specs = (
        P(None, None, "ctx", None),
        P("section", "ctx", None, "tp"),
        P("section", "tp", "ctx"),
        P("section", "ctx", "tp"),
        P("section", "tp", "ctx"),
        P("section", None, "ctx"),
        P("section", None, "ctx"),
        P("section", None, ("tp", "ctx")),
        P("section", ("tp", "ctx")),
        P(),
        P(None, None, "ctx", None),
    )
    out_specs = (
        P("section", None, None, "ctx", None),
        P("section", None, None, "ctx", None),
        P("section", "ctx", None, "tp"),
        P("section", "tp", "ctx"),
        P("section", "ctx", "tp"),
        P("section", "tp", "ctx"),
        P("section", None, "ctx"),
        P("section", None, "ctx"),
        P("section", None, ("tp", "ctx")),
        P("section", ("tp", "ctx")),
    )
    return jax.shard_map(
        on_device, mesh=mesh, in_specs=in_specs, out_specs=out_specs, check_vma=False
    )
```

```python
import functools

import jax
import jax.numpy as jnp
import numpy as np
from jax import lax
from jax.experimental import pallas as pl
from jax.experimental.pallas import tpu as pltpu
from jax.sharding import PartitionSpec as P

MESH = pl.DeviceIdType.MESH
f32 = jnp.float32
bf16 = jnp.bfloat16
epsilon = 1e-05
negative = -1e30

D = 768
SHARD = 48
QUARTER = 48
BLOCK = 96
ROWS = 192
KEYS = 1536
Q0, KV0, OUT0, UP0, DOWN0, WIDE = 0, 256, 640, 896, 1664, 2432
HALF = 1280
PIECE = 256
HEADS3 = 3
VMEM_LIMIT = 60 * 1024 * 1024


def where_am_i():
    s = lax.axis_index("section")
    c = lax.axis_index("ctx")
    t = lax.axis_index("tp")
    y = lax.div(c, 4)
    zh = lax.rem(lax.div(c, 2), 2)
    core = lax.rem(c, 2)
    return y, zh * 2 + s, core, t


def ident(y, z, core, t):
    return {"section": lax.rem(z, 2), "ctx": y * 4 + lax.div(z, 2) * 2 + core, "tp": t}


def ring(i, d):
    return lax.rem(i + d, 4)


def greet(peers):
    barrier = pltpu.get_barrier_semaphore()
    for peer in peers:
        pl.semaphore_signal(barrier, inc=1, device_id=peer, device_id_type=MESH)
    pl.semaphore_wait(barrier, len(peers))


def remote(src, dst, send, recv, peer):
    return pltpu.make_async_remote_copy(
        src_ref=src, dst_ref=dst, send_sem=send, recv_sem=recv, device_id=peer, device_id_type=MESH
    )


def dot(a, b):
    return lax.dot_general(a, b, (((1,), (0,)), ((), ())), preferred_element_type=f32)


def dot_t(a, b):
    return lax.dot_general(a, b, (((1,), (1,)), ((), ())), preferred_element_type=f32)


def hat(v):
    center = v - jnp.mean(v, axis=-1, keepdims=True)
    r = lax.rsqrt(jnp.mean(center * center, axis=-1, keepdims=True) + epsilon)
    return center * r, r


def norm(v, gain, shift):
    return hat(v)[0] * gain + shift


def norm_back(v, gain, c):
    vhat, r = hat(v)
    cg = c * gain
    grad = r * (
        cg - jnp.mean(cg, axis=-1, keepdims=True) - vhat * jnp.mean(cg * vhat, axis=-1, keepdims=True)
    )
    return grad, jnp.sum(c * vhat, axis=0, keepdims=True), jnp.sum(c, axis=0, keepdims=True)


def layers_kernel(
    pack_ref, f_ref, og_ref, keep_ref, sel_ref,
    own_ref, tile_ref, dist_ref,
    w_ref, grads, x_all, g_all, kept, n1, n2, gdi0, ga, rs, part, kv, att, act, slope, mid, lse, q, small,
    scores, acc, dkv, dqkv, core_in, y_in, little,
    cin_a, cin_b, s_a, s_b, zin_a, zin_b, u_a, u_b, yin_a, yin_b, tiles,
    x_send, x_recv, k_send, k_recv, b_send, b_recv, w_send, w_recv, r_send, r_recv, f_send, f_recv,
    d_send, d_recv, d_local, t_send, t_recv,
):
    y, z, core, t = where_am_i()
    other = 1 - core
    zh = lax.div(z, 2)
    mate = ident(y, z, other, t)

    def along_x(d):
        return ident(y, z, core, ring(t, d))

    def along_y(d):
        return ident(ring(y, d), z, core, t)

    def along_z(d):
        return ident(y, ring(z, d), core, t)

    greet(
        [ident(y, ring(z, a), core, ring(t, b)) for a in range(4) for b in range(4) if a or b]
        + [along_y(d) for d in (1, 2, 3)]
        + [mate]
    )
    later = []

    def put(src, dst, send, recv, to, when=None):
        def make():
            return remote(src, dst, send, recv, to)

        if when is None:
            make().start()
        else:
            pl.when(when)(lambda: make().start())
        later.append((when, make))

    def got(region, send, recv):
        remote(region, region, send, recv, mate).wait_recv()


    def cols(half):
        return pl.ds(0, UP0) if half == 0 else pl.ds(UP0, WIDE - UP0)

    first_core, second_core = core == 0, core == 1

    def holds(l):
        return lax.rem(z, 2) == l

    def lacks(l):
        return lax.rem(z, 2) != l

    def w_sems(l, half, i):
        return w_send.at[2 * l + half, i], w_recv.at[2 * l + half, i]

    def gather_a(l, half):
        here = w_ref.at[l, y, zh, core, :, cols(half)]
        src = pack_ref.at[:, cols(half)]
        for d in (1, 3, 2):
            put(src, here, *w_sems(l, half, d - 1), along_z(d), when=first_core & holds(l))
            put(src, here, *w_sems(l, half, d - 1), along_y(d), when=second_core & holds(l))

        @pl.when(holds(l))
        def _():
            w_ref[l, y, zh, core, :, cols(half)] = pack_ref[:, cols(half)]

    def from_z(d):
        return lax.div(ring(z, 4 - d), 2)

    def gather_b(l, half):
        c = cols(half)

        @pl.when(first_core & holds(l))
        def _():
            got(w_ref.at[l, y, from_z(2), core, :, c], *w_sems(l, half, 1))

        @pl.when(first_core & lacks(l))
        def _():
            for d in (1, 3):
                got(w_ref.at[l, y, from_z(d), core, :, c], *w_sems(l, half, d - 1))

        @pl.when(second_core & holds(l))
        def _():
            for d in (1, 3, 2):
                got(w_ref.at[l, ring(y, 4 - d), zh, core, :, c], *w_sems(l, half, d - 1))

        pair = w_ref.at[l, y, :, core, :, c]
        four = w_ref.at[l, :, zh, core, :, c]
        for d in (1, 3, 2):
            put(pair, pair, *w_sems(l, half, 2 + d), along_y(d), when=first_core)
            put(four, four, *w_sems(l, half, 2 + d), along_z(d), when=second_core & holds(l))

    def gather_c(l, half):
        c = cols(half)

        @pl.when(first_core)
        def _():
            for d in (1, 3, 2):
                got(w_ref.at[l, ring(y, 4 - d), :, core, :, c], *w_sems(l, half, 2 + d))

        @pl.when(second_core & holds(l))
        def _():
            got(w_ref.at[l, :, from_z(2), core, :, c], *w_sems(l, half, 4))

        @pl.when(second_core & lacks(l))
        def _():
            for d in (1, 3):
                got(w_ref.at[l, :, from_z(d), core, :, c], *w_sems(l, half, 2 + d))

        mine = w_ref.at[l, :, :, core, :, c]
        put(mine, mine, *w_sems(l, half, 6), mate)

    def gather_d(l, half):
        got(w_ref.at[l, :, :, other, :, cols(half)], *w_sems(l, half, 6))

    def weight(l, first, last):
        return w_ref[l, :, :, :, :, first:last].reshape(D, last - first)


    cin, s_out, zin, u_out, yin = (cin_b, cin_a), (s_b, s_a), (zin_b, zin_a), (u_b, u_a), (yin_b, yin_a)

    def r_sems(l, half, i):
        return r_send.at[2 * l + half, i], r_recv.at[2 * l + half, i]

    def keep_grad(l, first, value):
        n = value.shape[1]
        grads[l, :, :, :, :, first : first + n] = value.astype(bf16).reshape(4, 2, 2, SHARD, n)

    def scatter_a(l, half):
        put(grads.at[l, :, :, other, :, cols(half)], cin[half].at[l], *r_sems(l, half, 0), mate)

    def scatter_b(l, half):
        got(cin[half].at[l], *r_sems(l, half, 0))

        def add(i, carry):
            for b in range(2):
                s_out[half][l, i, b] = (
                    grads[l, i, b, core, :, cols(half)].astype(f32) + cin[half][l, i, b].astype(f32)
                ).astype(bf16)
            return carry

        lax.fori_loop(0, 4, add, 0)
        for d in (1, 3, 2):
            put(s_out[half].at[l, :, lax.div(ring(z, d), 2)], zin[half].at[d - 1], *r_sems(l, half, d),
                along_z(d), when=holds(l) if d == 2 else lacks(l))

    def scatter_c(l, half):
        @pl.when(holds(l))
        def _():
            for d in (1, 3, 2):
                got(zin[half].at[d - 1], *r_sems(l, half, d))

            def add(i, carry):
                total = s_out[half][l, i, zh].astype(f32)
                for d in (1, 2, 3):
                    total = total + zin[half][d - 1, i].astype(f32)
                u_out[half][i] = total.astype(bf16)
                return carry

            lax.fori_loop(0, 4, add, 0)

        for d in (2, 1, 3):
            put(u_out[half].at[ring(y, d)], yin[half].at[d - 1], *r_sems(l, half, 3 + d), along_y(d),
                when=holds(l))

    def scatter_d(l, half):
        @pl.when(holds(l))
        def _():
            total = u_out[half][y].astype(f32)
            for d in (1, 3, 2):
                got(yin[half].at[d - 1], *r_sems(l, half, 3 + d))
                total = total + yin[half][d - 1].astype(f32)
            own_ref[:, cols(half)] = total


    h = lax.div(t, 2)

    def place(l, kind):
        to_z = h * 2 + l
        dst = dist_ref.at[z, lax.rem(t, 2), kind]
        for a in range(4):
            here = jnp.logical_and(to_z == z, t == a)
            put(kept.at[l, kind], dst, d_send.at[2 * l + kind, a], d_recv.at[z, lax.rem(t, 2), kind],
                ident(y, to_z, core, a), when=jnp.logical_not(here))

        def make():
            return pltpu.make_async_copy(kept.at[l, kind], dst, d_local.at[kind])

        pl.when(to_z == z)(lambda: make().start())
        placed.append((to_z == z, make))

    placed = []


    quarter = pl.ds(pl.multiple_of(t * QUARTER, QUARTER), QUARTER)

    def rows_of(i):
        return pl.ds(pl.multiple_of(i * QUARTER, QUARTER), QUARTER)

    def share_start(phase, ref):
        for d in (1, 3, 2):
            put(ref.at[quarter], ref.at[quarter], x_send.at[phase, d - 1], x_recv.at[phase, d - 1], along_x(d))

    def share_wait(phase, ref):
        for d in (1, 3, 2):
            got(ref.at[rows_of(ring(t, 4 - d))], x_send.at[phase, d - 1], x_recv.at[phase, d - 1])

    def sum_start(phase, i):
        for d in (1, 3, 2):
            put(part.at[i, rows_of(ring(t, d))], rs.at[i, d - 1], x_send.at[phase, d - 1],
                x_recv.at[phase, d - 1], along_x(d))

    def sum_wait(phase, i):
        total = part[i, quarter, :].astype(f32)
        for d in (1, 3, 2):
            got(rs.at[i, d - 1], x_send.at[phase, d - 1], x_recv.at[phase, d - 1])
            total = total + rs[i, d - 1].astype(f32)
        return total


    col = lax.broadcasted_iota(jnp.int32, (1, 256), 1)
    q_masks = [jnp.where((col >= 64 * i) & (col < 64 * i + 64), 1.0, 0.0).astype(f32) for i in range(3)]
    v_masks = [jnp.where((col >= 64 * i + 64) & (col < 64 * i + 128), 1.0, 0.0).astype(f32) for i in range(3)]

    def by_head(rows, masks):
        rows = rows.astype(f32)
        return jnp.concatenate([rows * m for m in masks], axis=0)

    def from_heads(rows, masks):
        return sum(rows[i * ROWS : (i + 1) * ROWS] * masks[i] for i in range(3))

    def key_rows(b):
        return pl.ds(pl.multiple_of(b * ROWS, ROWS), ROWS)

    def attend(l, meanwhile):
        def sems(i):
            return k_send.at[l, i], k_recv.at[l, i]

        own = y * 2 + core
        for d in (1, 3, 2):
            put(kv.at[l, own], kv.at[l, own], *sems(d - 1), along_y(d))
        put(kv.at[l, own], kv.at[l, own], *sems(3), mate)
        meanwhile()
        q3 = by_head(q[l], q_masks).astype(bf16)

        def first(b, top):
            s = dot_t(kv[l, b, :, 0:256], q3)
            s = jnp.where(keep_ref[key_rows(b), :] < 0, negative, s)
            scores[key_rows(b), :] = s
            return jnp.maximum(top, jnp.max(s, axis=0, keepdims=True))

        top = first(own, jnp.full((1, 3 * ROWS), negative, f32))
        got(kv.at[l, y * 2 + other], *sems(3))
        top = first(y * 2 + other, top)

        def same_core(i, top):
            d = 1 + 2 * i - 3 * lax.div(i, 2)
            b = ring(y, 4 - d) * 2 + core
            got(kv.at[l, b], *sems(d - 1))
            remote(kv.at[l, b], kv.at[l, b], *sems(3 + d), mate).start()
            return first(b, top)

        top = lax.fori_loop(0, 3, same_core, top)
        for d in (1, 2, 3):
            b = ring(y, 4 - d) * 2 + core
            later.append((None, functools.partial(remote, kv.at[l, b], kv.at[l, b], *sems(3 + d), mate)))

        def other_core(i, top):
            d = 1 + 2 * i - 3 * lax.div(i, 2)
            b = ring(y, 4 - d) * 2 + other
            got(kv.at[l, b], *sems(3 + d))
            return first(b, top)

        top = lax.fori_loop(0, 3, other_core, top)
        acc[...] = jnp.zeros_like(acc)

        def second(b, total):
            p = jnp.exp(scores[key_rows(b), :] - top)
            acc[...] += dot(kv[l, b, :, 128:384].T, p.astype(bf16))
            return total + jnp.sum(p, axis=0, keepdims=True)

        total = lax.fori_loop(0, 8, second, jnp.zeros((1, 3 * ROWS), f32))
        lse[l] = top + jnp.log(total)
        att[l] = from_heads((acc[...] / total).T, v_masks).astype(bf16)

    def attend_back(l, grad_att, meanwhile):
        def sems(i):
            return b_send.at[l, i], b_recv.at[l, i]

        q3 = by_head(q[l], q_masks).astype(bf16)
        do3 = by_head(grad_att, v_masks)
        delta = jnp.sum((do3 * by_head(att[l], v_masks)).T, axis=0, keepdims=True)
        do3 = do3.astype(bf16)
        acc[...] = jnp.zeros_like(acc)
        log_total = lse[l]

        def block(b):
            k = kv[l, b, :, 0:256]
            s = jnp.where(keep_ref[key_rows(b), :] < 0, negative, dot_t(k, q3))
            p = jnp.exp(s - log_total)
            ds = (p * (dot_t(kv[l, b, :, 128:384], do3) - delta)).astype(bf16)
            dk = dot(ds, q3)
            dv = dot(p.astype(bf16), do3)
            acc[...] += dot(k.T, ds)
            return jnp.concatenate([dk[:, :128], dk[:, 128:] + dv[:, :128], dv[:, 128:]], axis=1)

        def for_mate(i, carry):
            off = 3 - i
            b = ring(y, off) * 2 + other
            dkv[l, b] = block(b).astype(bf16)
            remote(dkv.at[l, b], core_in.at[l, off], *sems(off), mate).start()
            return carry

        def for_y(i, carry):
            off = 3 - i
            b = ring(y, off) * 2 + core
            value = block(b)
            got(core_in.at[l, off], *sems(off))
            dkv[l, b] = (value + core_in[l, off].astype(f32)).astype(bf16)
            remote(dkv.at[l, b], y_in.at[l, off - 1], *sems(3 + off), along_y(off)).start()
            return carry

        lax.fori_loop(0, 4, for_mate, 0)
        lax.fori_loop(0, 3, for_y, 0)
        for off in range(4):
            b = ring(y, off) * 2 + other
            later.append((None, functools.partial(remote, dkv.at[l, b], core_in.at[l, off], *sems(off), mate)))
        for off in (1, 2, 3):
            b = ring(y, off) * 2 + core
            later.append((None, functools.partial(
                remote, dkv.at[l, b], y_in.at[l, off - 1], *sems(3 + off), along_y(off))))
        total = block(y * 2 + core)
        dqkv[l, :, 0:256] = (from_heads(acc[...].T, q_masks) * 0.125).astype(bf16)
        got(core_in.at[l, 0], *sems(0))
        total = total + core_in[l, 0].astype(f32)
        meanwhile()
        for off in (1, 3, 2):
            got(y_in.at[l, off - 1], *sems(3 + off))
            total = total + y_in[l, off - 1].astype(f32)
        dqkv[l, :, 256:640] = total.astype(bf16)


    def load_small(l):
        small[l] = weight(l, OUT0, OUT0 + 128).astype(f32).T[:16]

    def forward(l, x_q, on_kv, on_sum, on_share, on_last):
        row = small[l]
        bias = dot(row.astype(bf16), sel_ref[...])
        wide = dot(n1[l], weight(l, Q0, OUT0))
        kv[l, y * 2 + core] = (wide[:, 256:] + bias[8:9, 256:]).astype(bf16)
        q[l] = ((wide[:, :256] + bias[7:8, :256]).astype(bf16).astype(f32) * 0.125).astype(bf16)
        attend(l, on_kv)
        part[2 * l] = dot_t(att[l], weight(l, OUT0, UP0)).astype(bf16)
        sum_start(4 * l, 2 * l)
        on_sum()
        m = x_q + sum_wait(4 * l, 2 * l) + row[4:5]
        mid[l] = m
        n2[l, quarter, :] = norm(m, row[1:2], row[3:4]).astype(bf16)
        share_start(4 * l + 1, n2.at[l])
        on_share()
        share_wait(4 * l + 1, n2.at[l])
        u = dot(n2[l], weight(l, UP0, DOWN0)) + row[6:7]
        phi = 0.5 * (1.0 + lax.erf(u * np.float32(0.5**0.5)))
        act[l] = (u * phi).astype(bf16)
        part[2 * l + 1] = dot_t(act[l], weight(l, DOWN0, WIDE)).astype(bf16)
        sum_start(4 * l + 2, 2 * l + 1)
        slope[l] = phi + u * jnp.exp(-0.5 * u * u) * np.float32((2 * np.pi) ** -0.5)
        on_last()
        out = m + sum_wait(4 * l + 2, 2 * l + 1) + row[5:6]
        kept[l, 0] = out.astype(bf16)
        return out

    def backward(l, dout_q, gdi_ref, x_q, on_sum, on_share, on_att, on_last):
        base = 8 + 4 * (1 - l)
        row = small[l]
        gdi = gdi_ref[...]
        gpre = (dot(gdi, weight(l, DOWN0, WIDE)) * slope[l]).astype(bf16)
        part[4 + 2 * l] = dot_t(gpre, weight(l, UP0, DOWN0)).astype(bf16)
        sum_start(base, 4 + 2 * l)
        keep_grad(l, UP0, dot(n2[l].T, gpre))
        keep_grad(l, DOWN0, dot(gdi.T, act[l]))
        little[l] = jnp.zeros_like(little[l])
        little[l, 6:7, :] = jnp.sum(gpre.astype(f32), axis=0, keepdims=True)
        little[l, 5:6, :] = jnp.sum(dout_q, axis=0, keepdims=True)
        on_sum()
        c = sum_wait(base, 4 + 2 * l)
        gv, g_gain, g_shift = norm_back(mid[l], row[1:2], c)
        gm = dout_q + gv
        low = gm.astype(bf16)
        ga[l, quarter, :] = low
        share_start(base + 1, ga.at[l])
        little[l, 1:2, :] = g_gain
        little[l, 3:4, :] = g_shift
        little[l, 4:5, :] = jnp.sum(low.astype(f32), axis=0, keepdims=True)
        on_share()
        share_wait(base + 1, ga.at[l])
        attend_back(l, dot(ga[l], weight(l, OUT0, UP0)).astype(bf16), on_att)
        part[5 + 2 * l] = dot_t(dqkv[l], weight(l, Q0, OUT0)).astype(bf16)
        sum_start(base + 2, 5 + 2 * l)
        keep_grad(l, Q0, dot(n1[l].T, dqkv[l]))
        sums = jnp.sum(dqkv[l].astype(f32), axis=0, keepdims=True)
        wide_col = lax.broadcasted_iota(jnp.int32, (8, 640), 1)
        which = lax.broadcasted_iota(jnp.int32, (8, 640), 0)
        two = jnp.where(((wide_col < 256) & (which == 0)) | ((wide_col >= 256) & (which == 1)), sums, 0.0)
        placed_rows = dot_t(two.astype(bf16), sel_ref[...])
        little[l, 7:9, :] = placed_rows[0:2]
        on_last()
        c = sum_wait(base + 2, 5 + 2 * l)
        gv, g_gain, g_shift = norm_back(x_q, row[0:1], c)
        little[l, 0:1, :] = g_gain
        little[l, 2:3, :] = g_shift
        gx = gm + gv
        kept[l, 1] = gx.astype(bf16)
        return gx

    def out_grads(l):
        both = dot(ga[l].T, att[l])
        keep_grad(l, OUT0, jnp.concatenate([both[:, :128] + little[l].T, both[:, 128:]], axis=1))


    A, B = 1, 0
    gather_a(0, B)
    twin = ident(y, 3 - z, core, t)
    mine = pl.ds(pl.multiple_of(zh * BLOCK, BLOCK), BLOCK)
    theirs = pl.ds(pl.multiple_of((1 - zh) * BLOCK, BLOCK), BLOCK)
    put(f_ref.at[3 - z], x_all.at[mine], f_send.at[0], f_recv.at[0], twin)
    gather_a(0, A)
    put(og_ref.at[3 - z], g_all.at[mine], f_send.at[1], f_recv.at[1], twin)
    x_all[mine, :] = f_ref[z]
    g_all[mine, :] = og_ref[z]
    gather_b(0, B)
    gather_c(0, B)
    gather_b(0, A)
    got(x_all.at[theirs], f_send.at[0], f_recv.at[0])
    gather_d(0, B)
    load_small(0)
    n1[0] = norm(x_all[...].astype(f32), small[0, 0:1, :], small[0, 2:3, :]).astype(bf16)
    x0 = x_all[quarter, :].astype(f32)

    def run(*steps):
        def body():
            for step in steps:
                step[0](*step[1:])

        return body

    x1 = forward(
        0, x0,
        run((gather_c, 0, A), (gather_a, 1, B), (gather_a, 1, A)),
        run((gather_d, 0, A), (gather_b, 1, B)),
        run((gather_b, 1, A)),
        run((gather_c, 1, B), (gather_c, 1, A)),
    ).astype(bf16).astype(f32)
    gather_d(1, B)
    load_small(1)
    n1[1, quarter, :] = norm(x1, small[1, 0:1, :], small[1, 2:3, :]).astype(bf16)
    share_start(3, n1.at[1])
    share_wait(3, n1.at[1])
    forward(1, x1, run((place, 0, 0)), run((gather_d, 1, A)), run(), run())
    got(g_all.at[theirs], f_send.at[1], f_recv.at[1])
    gx = backward(
        1, g_all[quarter, :].astype(f32), g_all, x1,
        run((scatter_a, 1, A)), run((scatter_b, 1, A)), run((place, 1, 0)), run((scatter_c, 1, A)),
    ).astype(bf16)
    gdi0[quarter, :] = gx
    share_start(11, gdi0)
    out_grads(1)
    scatter_a(1, B)
    share_wait(11, gdi0)
    backward(
        0, gx.astype(f32), gdi0, x0,
        run((scatter_a, 0, A), (scatter_b, 1, B)), run((scatter_b, 0, A)), run((place, 1, 1)),
        run((scatter_c, 0, A), (scatter_c, 1, B)),
    )
    out_grads(0)
    scatter_a(0, B)
    place(0, 1)
    scatter_d(1, A)
    scatter_d(0, A)
    scatter_b(0, B)
    scatter_d(1, B)
    scatter_c(0, B)
    scatter_d(0, B)
    tiles[0] = own_ref[:, OUT0 : OUT0 + 128]
    for d in (1, 2, 3):
        put(tiles.at[0], tiles.at[d], t_send.at[d - 1], t_recv.at[d - 1], along_x(d))
    tile = tiles[0]
    for d in (1, 2, 3):
        got(tiles.at[d], t_send.at[d - 1], t_recv.at[d - 1])
        tile = tile + tiles[d]
    tile_ref[...] = tile
    for kind in range(2):
        for zz in range(4):
            for b in range(2):
                away = jnp.logical_not(jnp.logical_and(zz == z, t == zh * 2 + b))

                @pl.when(away)
                def _():
                    got(dist_ref.at[zz, b, kind], d_send.at[0, 0], d_recv.at[zz, b, kind])

    for when, make in placed:
        pl.when(when)(lambda: make().wait())
    for when, make in later:
        if when is None:
            make().wait_send()
        else:
            pl.when(when)(lambda: make().wait_send())


def layers_call(packed, frames, out_grad, keep, sel):
    vmem = pl.BlockSpec(memory_space=pltpu.VMEM)
    wide_a, wide_b = WIDE - UP0, UP0
    dma = pltpu.SemaphoreType.DMA
    return pl.pallas_call(
        layers_kernel,
        out_shape=(
            jax.ShapeDtypeStruct((SHARD, WIDE), f32),
            jax.ShapeDtypeStruct((SHARD, 128), f32),
            jax.ShapeDtypeStruct((4, 2, 2, QUARTER, D), bf16),
        ),
        in_specs=[vmem] * 5,
        out_specs=(vmem, vmem, pl.BlockSpec(memory_space=pl.ANY)),
        scratch_shapes=[
            pltpu.VMEM((2, 4, 2, 2, SHARD, WIDE), bf16),
            pltpu.VMEM((2, 4, 2, 2, SHARD, WIDE), bf16),
            pltpu.VMEM((ROWS, D), bf16),
            pltpu.VMEM((ROWS, D), bf16),
            pltpu.VMEM((2, 2, QUARTER, D), bf16),
            pltpu.VMEM((2, ROWS, D), bf16),
            pltpu.VMEM((2, ROWS, D), bf16),
            pltpu.VMEM((ROWS, D), bf16),
            pltpu.VMEM((2, ROWS, D), bf16),
            pltpu.VMEM((8, 3, QUARTER, D), bf16),
            pltpu.VMEM((8, ROWS, D), bf16),
            pltpu.VMEM((2, 8, ROWS, 384), bf16),
            pltpu.VMEM((2, ROWS, 256), bf16),
            pltpu.VMEM((2, ROWS, D), bf16),
            pltpu.VMEM((2, ROWS, D), f32),
            pltpu.VMEM((2, QUARTER, D), f32),
            pltpu.VMEM((2, 1, 3 * ROWS), f32),
            pltpu.VMEM((2, ROWS, 256), bf16),
            pltpu.VMEM((2, 16, D), f32),
            pltpu.VMEM((KEYS, 3 * ROWS), f32),
            pltpu.VMEM((256, 3 * ROWS), f32),
            pltpu.VMEM((2, 8, ROWS, 384), bf16),
            pltpu.VMEM((2, ROWS, 640), bf16),
            pltpu.VMEM((2, 4, ROWS, 384), bf16),
            pltpu.VMEM((2, 3, ROWS, 384), bf16),
            pltpu.VMEM((2, 128, D), f32),
            pltpu.VMEM((2, 4, 2, SHARD, wide_a), bf16),
            pltpu.VMEM((2, 4, 2, SHARD, wide_b), bf16),
            pltpu.VMEM((2, 4, 2, SHARD, wide_a), bf16),
            pltpu.VMEM((2, 4, 2, SHARD, wide_b), bf16),
            pltpu.VMEM((3, 4, SHARD, wide_a), bf16),
            pltpu.VMEM((3, 4, SHARD, wide_b), bf16),
            pltpu.VMEM((4, SHARD, wide_a), bf16),
            pltpu.VMEM((4, SHARD, wide_b), bf16),
            pltpu.VMEM((3, SHARD, wide_a), bf16),
            pltpu.VMEM((3, SHARD, wide_b), bf16),
            pltpu.VMEM((4, SHARD, 128), f32),
            dma((16, 3)), dma((16, 3)),
            dma((2, 7)), dma((2, 7)),
            dma((2, 7)), dma((2, 7)),
            dma((4, 7)), dma((4, 7)),
            dma((4, 7)), dma((4, 7)),
            dma((2,)), dma((2,)),
            dma((4, 4)), dma((4, 2, 2)), dma((2,)),
            dma((3,)), dma((3,)),
        ],
        compiler_params=pltpu.CompilerParams(
            collective_id=0, has_side_effects=True, vmem_limit_bytes=VMEM_LIMIT
        ),
        name="layers",
    )(packed, frames, out_grad, keep, sel)


def selection():
    sel = np.zeros((D, 640), np.float32)
    for c in range(16):
        for i in range(12):
            sel[c * 48 + i, c * 12 + i] = 1.0
            sel[c * 48 + i, 448 + c * 12 + i] = 1.0
    return sel


def key_frames():
    r = np.arange(KEYS)
    j, w = r // ROWS, r % ROWS
    y, core = j // 2, j % 2
    hi = w // BLOCK
    return (((y * 2 + hi) * 2 + core) * BLOCK + w % BLOCK).astype(np.int32)


def on_device(
    frames, w_qkv, w_out, w_up, w_down, ln_gains, shifts, qv_bias, up_bias, lengths, out_grad
):
    _, z, _, _ = where_am_i()
    pad = ((0, 0), (0, SHARD - 12))
    little = jnp.concatenate(
        [ln_gains[0], shifts[0], up_bias, jnp.pad(qv_bias[0], pad), jnp.zeros((55, SHARD), bf16)], axis=0
    )
    packed = jnp.concatenate(
        [
            w_qkv[0, :, 0], jnp.zeros((SHARD, 64), bf16), w_qkv[0, :, 1], w_qkv[0, :, 2],
            little.T, w_out[0].T, w_up[0], w_down[0].T,
        ],
        axis=1,
    )
    length = lax.dynamic_index_in_dim(lengths, z, 0, keepdims=False)[0]
    keep = jnp.where(jnp.asarray(key_frames())[:, None] < length, 0.0, -1.0).astype(f32)
    own, tile, dist = layers_call(
        packed, frames[:, 0], out_grad[:, 0], keep, jnp.asarray(selection(), bf16)
    )
    outs = dist.astype(f32)
    tile_t = tile.T
    little_t = own[:, OUT0 : OUT0 + 64].T
    grad_qkv = jnp.stack([own[:, 0:192], own[:, 256:448], own[:, 448:640]], axis=1)
    return (
        outs[:, :, 0].reshape(1, 4, 1, BLOCK, D),
        outs[:, :, 1].reshape(1, 4, 1, BLOCK, D),
        grad_qkv[None],
        own[:, OUT0 + 64 : UP0].T[None],
        own[:, UP0:DOWN0][None],
        own[:, DOWN0:WIDE].T[None],
        tile_t[0:2][None],
        tile_t[2:6][None],
        little_t[7:9, :12][None],
        little_t[6:7],
    )


def solution(mesh):
    in_specs = (
        P(None, None, "ctx", None),
        P("section", "ctx", None, "tp"),
        P("section", "tp", "ctx"),
        P("section", "ctx", "tp"),
        P("section", "tp", "ctx"),
        P("section", None, "ctx"),
        P("section", None, "ctx"),
        P("section", None, ("tp", "ctx")),
        P("section", ("tp", "ctx")),
        P(),
        P(None, None, "ctx", None),
    )
    out_specs = (
        P("section", None, None, "ctx", None),
        P("section", None, None, "ctx", None),
        P("section", "ctx", None, "tp"),
        P("section", "tp", "ctx"),
        P("section", "ctx", "tp"),
        P("section", "tp", "ctx"),
        P("section", None, "ctx"),
        P("section", None, "ctx"),
        P("section", None, ("tp", "ctx")),
        P("section", ("tp", "ctx")),
    )
    return jax.shard_map(
        on_device, mesh=mesh, in_specs=in_specs, out_specs=out_specs, check_vma=False
    )
```

```python
import functools

import jax
import jax.numpy as jnp
import numpy as np
from jax import lax
from jax.experimental import pallas as pl
from jax.experimental.pallas import tpu as pltpu
from jax.sharding import PartitionSpec as P

MESH = pl.DeviceIdType.MESH
f32 = jnp.float32
bf16 = jnp.bfloat16
epsilon = 1e-05
negative = -1e30

D = 768
SHARD = 48
QUARTER = 48
BLOCK = 96
ROWS = 192
KEYS = 1536
Q0, KV0, OUT0, UP0, DOWN0, WIDE = 0, 256, 640, 896, 1664, 2432
HALF = 1280
PIECE = 256
HEADS3 = 3
VMEM_LIMIT = 60 * 1024 * 1024


def where_am_i():
    s = lax.axis_index("section")
    c = lax.axis_index("ctx")
    t = lax.axis_index("tp")
    y = lax.div(c, 4)
    zh = lax.rem(lax.div(c, 2), 2)
    core = lax.rem(c, 2)
    return y, zh * 2 + s, core, t


def ident(y, z, core, t):
    return {"section": lax.rem(z, 2), "ctx": y * 4 + lax.div(z, 2) * 2 + core, "tp": t}


def ring(i, d):
    return lax.rem(i + d, 4)


def greet(peers):
    barrier = pltpu.get_barrier_semaphore()
    for peer in peers:
        pl.semaphore_signal(barrier, inc=1, device_id=peer, device_id_type=MESH)
    pl.semaphore_wait(barrier, len(peers))


def remote(src, dst, send, recv, peer):
    return pltpu.make_async_remote_copy(
        src_ref=src, dst_ref=dst, send_sem=send, recv_sem=recv, device_id=peer, device_id_type=MESH
    )


def dot(a, b):
    return lax.dot_general(a, b, (((1,), (0,)), ((), ())), preferred_element_type=f32)


def dot_t(a, b):
    return lax.dot_general(a, b, (((1,), (1,)), ((), ())), preferred_element_type=f32)


def hat(v):
    center = v - jnp.mean(v, axis=-1, keepdims=True)
    r = lax.rsqrt(jnp.mean(center * center, axis=-1, keepdims=True) + epsilon)
    return center * r, r


def norm(v, gain, shift):
    return hat(v)[0] * gain + shift


def norm_back(v, gain, c):
    vhat, r = hat(v)
    cg = c * gain
    grad = r * (
        cg - jnp.mean(cg, axis=-1, keepdims=True) - vhat * jnp.mean(cg * vhat, axis=-1, keepdims=True)
    )
    return grad, jnp.sum(c * vhat, axis=0, keepdims=True), jnp.sum(c, axis=0, keepdims=True)


def layers_kernel(
    f_ref, wqkv_ref, wout_ref, wup_ref, wdown_ref, gains_ref, shifts_ref, qv_ref, up_ref, len_ref, og_ref,
    own_ref, tile_ref, dist_ref,
    pack_ref, turned, sel_ref, w_ref, grads, x_all, g_all, x1_all, o1_all, gx1_all, gx0_all, both, n1, n2, ga, rs, part, kv, att, act, slope, mid, lse, q, small,
    scores, acc, dkv, dqkv, core_in, y_in, little,
    cin_a, cin_b, s_a, s_b, zin_a, zin_b, u_a, u_b, yin_a, yin_b, tiles,
    x_send, x_recv, k_send, k_recv, b_send, b_recv, w_send, w_recv, r_send, r_recv, f_send, f_recv,
    d_send, d_recv, d_local, t_send, t_recv,
):
    y, z, core, t = where_am_i()
    other = 1 - core
    zh = lax.div(z, 2)
    mate = ident(y, z, other, t)

    def along_x(d):
        return ident(y, z, core, ring(t, d))

    def along_y(d):
        return ident(ring(y, d), z, core, t)

    def along_z(d):
        return ident(y, ring(z, d), core, t)

    greet(
        [along_x(d) for d in (1, 2, 3)]
        + [along_y(d) for d in (1, 2, 3)]
        + [along_z(d) for d in (1, 2, 3)]
        + [mate]
    )
    later = []


    turned[...] = jnp.zeros_like(turned)
    turned[0:2, 0:SHARD] = gains_ref[0].astype(f32)
    turned[2:6, 0:SHARD] = shifts_ref[0].astype(f32)
    turned[6:7, 0:SHARD] = up_ref[...].astype(f32)
    turned[7:9, 0:12] = qv_ref[0].astype(f32)
    pack_ref[:, OUT0:UP0] = jnp.concatenate(
        [turned[...].T[:SHARD, 0:64].astype(bf16), wout_ref[...]], axis=1
    )
    pack_ref[:, DOWN0:WIDE] = wdown_ref[...]
    pack_ref[:, UP0:DOWN0] = wup_ref[0]
    pack_ref[:, Q0:KV0] = jnp.concatenate([wqkv_ref[0], jnp.zeros((SHARD, 64), bf16)], axis=1)
    pack_ref[:, KV0:OUT0] = jnp.concatenate([wqkv_ref[1], wqkv_ref[2]], axis=1)

    def put(src, dst, send, recv, to, when=None):
        def make():
            return remote(src, dst, send, recv, to)

        if when is None:
            make().start()
        else:
            pl.when(when)(lambda: make().start())
        later.append((when, make))

    def got(region, send, recv):
        remote(region, region, send, recv, mate).wait_recv()


    def cols(half):
        return pl.ds(0, UP0) if half == 0 else pl.ds(UP0, WIDE - UP0)

    first_core, second_core = core == 0, core == 1

    def holds(l):
        return lax.rem(z, 2) == l

    def lacks(l):
        return lax.rem(z, 2) != l

    def w_sems(l, half, i):
        return w_send.at[2 * l + half, i], w_recv.at[2 * l + half, i]

    def gather_a(l, half):
        here = w_ref.at[l, y, zh, core, :, cols(half)]
        src = pack_ref.at[:, cols(half)]
        for d in (1, 3, 2):
            put(src, here, *w_sems(l, half, d - 1), along_z(d), when=first_core & holds(l))
            put(src, here, *w_sems(l, half, d - 1), along_y(d), when=second_core & holds(l))

        @pl.when(holds(l))
        def _():
            w_ref[l, y, zh, core, :, cols(half)] = pack_ref[:, cols(half)]

    def from_z(d):
        return lax.div(ring(z, 4 - d), 2)

    def gather_b(l, half):
        c = cols(half)

        @pl.when(first_core & holds(l))
        def _():
            got(w_ref.at[l, y, from_z(2), core, :, c], *w_sems(l, half, 1))

        @pl.when(first_core & lacks(l))
        def _():
            for d in (1, 3):
                got(w_ref.at[l, y, from_z(d), core, :, c], *w_sems(l, half, d - 1))

        @pl.when(second_core & holds(l))
        def _():
            for d in (1, 3, 2):
                got(w_ref.at[l, ring(y, 4 - d), zh, core, :, c], *w_sems(l, half, d - 1))

        pair = w_ref.at[l, y, :, core, :, c]
        four = w_ref.at[l, :, zh, core, :, c]
        for d in (1, 3, 2):
            put(pair, pair, *w_sems(l, half, 2 + d), along_y(d), when=first_core)
            put(four, four, *w_sems(l, half, 2 + d), along_z(d), when=second_core & holds(l))

    def gather_c(l, half):
        c = cols(half)

        @pl.when(first_core)
        def _():
            for d in (1, 3, 2):
                got(w_ref.at[l, ring(y, 4 - d), :, core, :, c], *w_sems(l, half, 2 + d))

        @pl.when(second_core & holds(l))
        def _():
            got(w_ref.at[l, :, from_z(2), core, :, c], *w_sems(l, half, 4))

        @pl.when(second_core & lacks(l))
        def _():
            for d in (1, 3):
                got(w_ref.at[l, :, from_z(d), core, :, c], *w_sems(l, half, 2 + d))

        mine = w_ref.at[l, :, :, core, :, c]
        put(mine, mine, *w_sems(l, half, 6), mate)

    def gather_d(l, half):
        got(w_ref.at[l, :, :, other, :, cols(half)], *w_sems(l, half, 6))

    def weight(l, first, last):
        return w_ref[l, :, :, :, :, first:last].reshape(D, last - first)


    pieces = {"ud": (UP0, WIDE, UP0, 1), "qkv": (Q0, OUT0, 0, 0), "out": (OUT0, UP0, 0, 0)}
    numbers = {"ud": 0, "qkv": 1, "out": 2}
    cin, s_out, zin, u_out, yin = (cin_b, cin_a), (s_b, s_a), (zin_b, zin_a), (u_b, u_a), (yin_b, yin_a)

    def r_sems(l, piece, i):
        return r_send.at[3 * l + numbers[piece], i], r_recv.at[3 * l + numbers[piece], i]

    def spans(piece):
        first, last, base, which = pieces[piece]
        return pl.ds(first, last - first), pl.ds(first - base, last - first), which

    def keep_grad(l, first, value):
        n = value.shape[1]
        grads[l, :, :, :, :, first : first + n] = value.astype(bf16).reshape(4, 2, 2, SHARD, n)

    def scatter_a(l, piece):
        wide, span, n = spans(piece)
        put(grads.at[l, :, :, other, :, wide], cin[n].at[l, :, :, :, span], *r_sems(l, piece, 0), mate)

    def scatter_b(l, piece):
        wide, span, n = spans(piece)
        got(cin[n].at[l, :, :, :, span], *r_sems(l, piece, 0))

        def add(i, carry):
            for b in range(2):
                s_out[n][l, i, b, :, span] = (
                    grads[l, i, b, core, :, wide].astype(f32) + cin[n][l, i, b, :, span].astype(f32)
                ).astype(bf16)
            return carry

        lax.fori_loop(0, 4, add, 0)
        for d in (2, 1, 3):
            put(s_out[n].at[l, :, lax.div(ring(z, d), 2), :, span], zin[n].at[d - 1, :, :, span],
                *r_sems(l, piece, d), along_z(d), when=holds(l) if d == 2 else lacks(l))

    def scatter_c(l, piece):
        wide, span, n = spans(piece)

        @pl.when(holds(l))
        def _():
            for d in (1, 3, 2):
                got(zin[n].at[d - 1, :, :, span], *r_sems(l, piece, d))

            def add(i, carry):
                total = s_out[n][l, i, zh, :, span].astype(f32)
                for d in (1, 2, 3):
                    total = total + zin[n][d - 1, i, :, span].astype(f32)
                u_out[n][i, :, span] = total.astype(bf16)
                return carry

            lax.fori_loop(0, 4, add, 0)

        for d in (2, 1, 3):
            put(u_out[n].at[ring(y, d), :, span], yin[n].at[d - 1, :, span], *r_sems(l, piece, 3 + d),
                along_y(d), when=holds(l))

    def scatter_d(l, piece):
        wide, span, n = spans(piece)

        @pl.when(holds(l))
        def _():
            total = u_out[n][y, :, span].astype(f32)
            for d in (1, 3, 2):
                got(yin[n].at[d - 1, :, span], *r_sems(l, piece, 3 + d))
                total = total + yin[n][d - 1, :, span].astype(f32)
            own_ref[:, wide] = total


    placed = []

    def place(l, kind, ref):
        for half in range(2):
            to_z = 2 * half + l
            src = ref.at[pl.ds(half * BLOCK, BLOCK)]
            dst = dist_ref.at[kind, z]
            put(src, dst, d_send.at[2 * l + kind, half], d_recv.at[kind, z], ident(y, to_z, core, t),
                when=z != to_z)
            make = functools.partial(pltpu.make_async_copy, src, dst, d_local.at[kind])
            start_here(z == to_z, make)
            placed.append((z == to_z, make))

    def start_here(when, make):
        pl.when(when)(lambda: make().start())


    quarter = pl.ds(pl.multiple_of(t * QUARTER, QUARTER), QUARTER)

    def rows_of(i):
        return pl.ds(pl.multiple_of(i * QUARTER, QUARTER), QUARTER)

    def share_start(phase, ref):
        for d in (1, 3, 2):
            put(ref.at[quarter], ref.at[quarter], x_send.at[phase, d - 1], x_recv.at[phase, d - 1], along_x(d))

    def share_wait(phase, ref):
        for d in (1, 3, 2):
            got(ref.at[rows_of(ring(t, 4 - d))], x_send.at[phase, d - 1], x_recv.at[phase, d - 1])

    def sum_start(phase, i):
        for d in (1, 3, 2):
            put(part.at[i, rows_of(ring(t, d))], rs.at[i, d - 1], x_send.at[phase, d - 1],
                x_recv.at[phase, d - 1], along_x(d))

    def sum_wait(phase, i):
        total = part[i, quarter, :].astype(f32)
        for d in (1, 3, 2):
            got(rs.at[i, d - 1], x_send.at[phase, d - 1], x_recv.at[phase, d - 1])
            total = total + rs[i, d - 1].astype(f32)
        return total


    col = lax.broadcasted_iota(jnp.int32, (1, 256), 1)
    q_masks = [jnp.where((col >= 64 * i) & (col < 64 * i + 64), 1.0, 0.0).astype(f32) for i in range(3)]
    v_masks = [jnp.where((col >= 64 * i + 64) & (col < 64 * i + 128), 1.0, 0.0).astype(f32) for i in range(3)]

    def by_head(rows, masks):
        rows = rows.astype(f32)
        return jnp.concatenate([rows * m for m in masks], axis=0)

    def from_heads(rows, masks):
        return sum(rows[i * ROWS : (i + 1) * ROWS] * masks[i] for i in range(3))

    length = len_ref[z, 0]
    within = lax.broadcasted_iota(jnp.int32, (ROWS, 1), 0)
    within = jnp.where(within >= BLOCK, within + BLOCK, within)

    def masked(b, s):
        first = (lax.div(b, 2) * 4 + lax.rem(b, 2)) * BLOCK
        return jnp.where(within < length - first, s, negative)

    def key_rows(b):
        return pl.ds(pl.multiple_of(b * ROWS, ROWS), ROWS)

    def send_keys(l):
        own = kv.at[l, y * 2 + core]
        for d in (1, 3, 2):
            put(own, own, k_send.at[l, d - 1], k_recv.at[l, d - 1], along_y(d))
        put(own, own, k_send.at[l, 3], k_recv.at[l, 3], mate)

    def attend(l, meanwhile):
        def sems(i):
            return k_send.at[l, i], k_recv.at[l, i]

        own = y * 2 + core
        q3 = by_head(q[l], q_masks).astype(bf16)

        def first(b, top):
            s = dot_t(kv[l, b, :, 0:256], q3)
            s = masked(b, s)
            scores[key_rows(b), :] = s
            return jnp.maximum(top, jnp.max(s, axis=0, keepdims=True))

        top = first(own, jnp.full((1, 3 * ROWS), negative, f32))
        got(kv.at[l, y * 2 + other], *sems(3))
        top = first(y * 2 + other, top)

        def same_core(i, top):
            d = 1 + 2 * i - 3 * lax.div(i, 2)
            b = ring(y, 4 - d) * 2 + core
            got(kv.at[l, b], *sems(d - 1))
            remote(kv.at[l, b], kv.at[l, b], *sems(3 + d), mate).start()
            return first(b, top)

        top = lax.fori_loop(0, 3, same_core, top)
        for d in (1, 2, 3):
            b = ring(y, 4 - d) * 2 + core
            later.append((None, functools.partial(remote, kv.at[l, b], kv.at[l, b], *sems(3 + d), mate)))

        def other_core(i, top):
            d = 1 + 2 * i - 3 * lax.div(i, 2)
            b = ring(y, 4 - d) * 2 + other
            got(kv.at[l, b], *sems(3 + d))
            return first(b, top)

        top = lax.fori_loop(0, 3, other_core, top)
        meanwhile()
        acc[...] = jnp.zeros_like(acc)

        def second(b, total):
            p = jnp.exp(scores[key_rows(b), :] - top)
            acc[...] += dot(kv[l, b, :, 128:384].T, p.astype(bf16))
            return total + jnp.sum(p, axis=0, keepdims=True)

        total = lax.fori_loop(0, 8, second, jnp.zeros((1, 3 * ROWS), f32))
        lse[l] = top + jnp.log(total)
        att[l] = from_heads((acc[...] / total).T, v_masks).astype(bf16)

    def attend_back(l, grad_att, meanwhile):
        def sems(i):
            return b_send.at[l, i], b_recv.at[l, i]

        q3 = by_head(q[l], q_masks).astype(bf16)
        do3 = by_head(grad_att, v_masks)
        delta = jnp.sum((do3 * by_head(att[l], v_masks)).T, axis=0, keepdims=True)
        do3 = do3.astype(bf16)
        acc[...] = jnp.zeros_like(acc)
        log_total = lse[l]

        def block(b):
            k = kv[l, b, :, 0:256]
            s = masked(b, dot_t(k, q3))
            p = jnp.exp(s - log_total)
            ds = (p * (dot_t(kv[l, b, :, 128:384], do3) - delta)).astype(bf16)
            dk = dot(ds, q3)
            dv = dot(p.astype(bf16), do3)
            acc[...] += dot(k.T, ds)
            return jnp.concatenate([dk[:, :128], dk[:, 128:] + dv[:, :128], dv[:, 128:]], axis=1)

        def for_mate(off):
            b = ring(y, off) * 2 + other
            dkv[l, b] = block(b).astype(bf16)
            remote(dkv.at[l, b], core_in.at[l, off], *sems(off), mate).start()

        def step(i, carry):
            off = 2 + i - 3 * lax.div(i, 2)
            for_mate(off)
            b = ring(y, off) * 2 + core
            value = block(b)
            got(core_in.at[l, off], *sems(off))
            dkv[l, b] = (value + core_in[l, off].astype(f32)).astype(bf16)
            remote(dkv.at[l, b], y_in.at[l, off - 1], *sems(3 + off), along_y(off)).start()
            return carry

        lax.fori_loop(0, 3, step, 0)
        for_mate(0)
        for off in range(4):
            b = ring(y, off) * 2 + other
            later.append((None, functools.partial(remote, dkv.at[l, b], core_in.at[l, off], *sems(off), mate)))
        for off in (1, 2, 3):
            b = ring(y, off) * 2 + core
            later.append((None, functools.partial(
                remote, dkv.at[l, b], y_in.at[l, off - 1], *sems(3 + off), along_y(off))))
        total = block(y * 2 + core)
        dqkv[l, :, 0:256] = (from_heads(acc[...].T, q_masks) * 0.125).astype(bf16)
        got(core_in.at[l, 0], *sems(0))
        total = total + core_in[l, 0].astype(f32)
        meanwhile()
        for off in (1, 3, 2):
            got(y_in.at[l, off - 1], *sems(3 + off))
            total = total + y_in[l, off - 1].astype(f32)
        dqkv[l, :, 256:640] = total.astype(bf16)


    def load_small(l):
        small[l] = weight(l, OUT0, OUT0 + 128).astype(f32).T[:16]

    def forward(l, x_q, on_kv, on_sum, on_share, on_last):
        row = small[l]
        bias = dot(row.astype(bf16), sel_ref[...])
        kv[l, y * 2 + core] = (dot(n1[l], weight(l, KV0, OUT0)) + bias[8:9, 256:]).astype(bf16)
        send_keys(l)
        queries = dot(n1[l], weight(l, Q0, KV0)) + bias[7:8, :256]
        q[l] = (queries.astype(bf16).astype(f32) * 0.125).astype(bf16)
        attend(l, on_kv)
        part[2 * l] = dot_t(att[l], weight(l, OUT0, UP0)).astype(bf16)
        sum_start(4 * l, 2 * l)
        on_sum()
        m = x_q + sum_wait(4 * l, 2 * l) + row[4:5]
        mid[l] = m
        n2[l, quarter, :] = norm(m, row[1:2], row[3:4]).astype(bf16)
        share_start(4 * l + 1, n2.at[l])
        on_share()
        share_wait(4 * l + 1, n2.at[l])
        gather_d(l, 1)
        u = dot(n2[l], weight(l, UP0, DOWN0)) + row[6:7]
        phi = 0.5 * (1.0 + lax.erf(u * np.float32(0.5**0.5)))
        act[l] = (u * phi).astype(bf16)
        part[2 * l + 1] = dot_t(act[l], weight(l, DOWN0, WIDE)).astype(bf16)
        sum_start(4 * l + 2, 2 * l + 1)
        slope[l] = phi + u * jnp.exp(-0.5 * u * u) * np.float32((2 * np.pi) ** -0.5)
        on_last()
        return (m + sum_wait(4 * l + 2, 2 * l + 1) + row[5:6]).astype(bf16)

    def backward(l, dout_q, gdi_ref, x_q, on_sum, on_share, on_att, on_last):
        base = 8 + 4 * (1 - l)
        row = small[l]
        gdi = gdi_ref[...]
        gpre = (dot(gdi, weight(l, DOWN0, WIDE)) * slope[l]).astype(bf16)
        part[4 + 2 * l] = dot_t(gpre, weight(l, UP0, DOWN0)).astype(bf16)
        sum_start(base, 4 + 2 * l)
        keep_grad(l, UP0, dot(n2[l].T, gpre))
        keep_grad(l, DOWN0, dot(gdi.T, act[l]))
        little[l] = jnp.zeros_like(little[l])
        little[l, 6:7, :] = jnp.sum(gpre.astype(f32), axis=0, keepdims=True)
        little[l, 5:6, :] = jnp.sum(dout_q, axis=0, keepdims=True)
        on_sum()
        c = sum_wait(base, 4 + 2 * l)
        gv, g_gain, g_shift = norm_back(mid[l], row[1:2], c)
        gm = dout_q + gv
        low = gm.astype(bf16)
        ga[l, quarter, :] = low
        share_start(base + 1, ga.at[l])
        little[l, 1:2, :] = g_gain
        little[l, 3:4, :] = g_shift
        little[l, 4:5, :] = jnp.sum(low.astype(f32), axis=0, keepdims=True)
        on_share()
        share_wait(base + 1, ga.at[l])
        attend_back(l, dot(ga[l], weight(l, OUT0, UP0)).astype(bf16), on_att)
        part[5 + 2 * l] = dot_t(dqkv[l], weight(l, Q0, OUT0)).astype(bf16)
        sum_start(base + 2, 5 + 2 * l)
        keep_grad(l, Q0, dot(n1[l].T, dqkv[l]))
        scatter_a(l, "qkv")
        sums = jnp.sum(dqkv[l].astype(f32), axis=0, keepdims=True)
        wide_col = lax.broadcasted_iota(jnp.int32, (8, 640), 1)
        which = lax.broadcasted_iota(jnp.int32, (8, 640), 0)
        two = jnp.where(((wide_col < 256) & (which == 0)) | ((wide_col >= 256) & (which == 1)), sums, 0.0)
        placed_rows = dot_t(two.astype(bf16), sel_ref[...])
        little[l, 7:9, :] = placed_rows[0:2]
        both[...] = dot(ga[l].T, att[l])
        on_last()
        c = sum_wait(base + 2, 5 + 2 * l)
        gv, g_gain, g_shift = norm_back(x_q, row[0:1], c)
        little[l, 0:1, :] = g_gain
        little[l, 2:3, :] = g_shift
        return (gm + gv).astype(bf16)

    def out_grads(l):
        keep_grad(l, OUT0, jnp.concatenate([both[:, :128] + little[l].T, both[:, 128:]], axis=1))


    A, B = 1, 0
    gather_a(0, B)
    twin = ident(y, 3 - z, core, t)
    mine = pl.ds(pl.multiple_of(zh * BLOCK, BLOCK), BLOCK)
    theirs = pl.ds(pl.multiple_of((1 - zh) * BLOCK, BLOCK), BLOCK)
    put(f_ref.at[3 - z, 0], x_all.at[mine], f_send.at[0], f_recv.at[0], twin)
    row, column = (lax.broadcasted_iota(jnp.int32, (SHARD, 640), i) for i in range(2))
    for i in range(16):
        hit = ((column == row + 12 * i) | (column == row + 12 * i + 448)) & (row < 12)
        sel_ref[i * SHARD : (i + 1) * SHARD, :] = jnp.where(hit, 1.0, 0.0).astype(bf16)
    x_all[mine, :] = f_ref[z, 0]
    g_all[mine, :] = og_ref[z, 0]
    gather_b(0, B)
    gather_a(0, A)
    put(og_ref.at[3 - z, 0], g_all.at[mine], f_send.at[1], f_recv.at[1], twin)
    gather_c(0, B)
    got(x_all.at[theirs], f_send.at[0], f_recv.at[0])
    gather_d(0, B)
    load_small(0)

    def run(*steps):
        def body():
            for step in steps:
                step[0](*step[1:])

        return body

    def start_layer(l, ref):
        n1[l] = norm(ref[...].astype(f32), small[l, 0:1, :], small[l, 2:3, :]).astype(bf16)
        return ref[quarter, :].astype(f32)

    x0 = start_layer(0, x_all)
    x1_all[quarter, :] = forward(
        0, x0,
        run((gather_b, 0, A)),
        run((gather_a, 1, B), (gather_a, 1, A)),
        run((gather_c, 0, A)),
        run((gather_b, 1, B)),
    )
    share_start(3, x1_all)
    gather_c(1, B)
    share_wait(3, x1_all)
    gather_d(1, B)
    load_small(1)
    x1 = start_layer(1, x1_all)
    o1_all[quarter, :] = forward(
        1, x1, run((gather_b, 1, A)), run((place, 0, 0, x1_all)), run((gather_c, 1, A)), run()
    )
    got(g_all.at[theirs], f_send.at[1], f_recv.at[1])
    gx1_all[quarter, :] = backward(
        1, g_all[quarter, :].astype(f32), g_all, x1,
        run((scatter_a, 1, "ud")), run((scatter_b, 1, "ud")), run((share_start, 7, o1_all)),
        run((scatter_c, 1, "ud")),
    )
    share_start(11, gx1_all)
    out_grads(1)
    scatter_a(1, "out")
    scatter_b(1, "qkv")
    share_wait(11, gx1_all)
    gx0_all[quarter, :] = backward(
        0, gx1_all[quarter, :].astype(f32), gx1_all, x0,
        run((scatter_a, 0, "ud"), (scatter_b, 1, "out")),
        run((scatter_b, 0, "ud")),
        run((place, 1, 1, gx1_all), (share_wait, 7, o1_all), (place, 1, 0, o1_all)),
        run((scatter_c, 1, "qkv"), (scatter_c, 1, "out"), (scatter_c, 0, "ud"), (scatter_b, 0, "qkv")),
    )
    out_grads(0)
    scatter_a(0, "out")
    share_start(15, gx0_all)
    for piece in ("ud", "qkv", "out"):
        scatter_d(1, piece)
    scatter_c(0, "qkv")
    scatter_b(0, "out")
    scatter_d(0, "ud")
    share_wait(15, gx0_all)
    place(0, 1, gx0_all)
    scatter_c(0, "out")
    scatter_d(0, "qkv")
    scatter_d(0, "out")
    tiles[0] = own_ref[:, OUT0 : OUT0 + 128]
    for d in (1, 2, 3):
        put(tiles.at[0], tiles.at[d], t_send.at[d - 1], t_recv.at[d - 1], along_x(d))
    tile = tiles[0]
    for d in (1, 2, 3):
        got(tiles.at[d], t_send.at[d - 1], t_recv.at[d - 1])
        tile = tile + tiles[d]
    tile_ref[...] = tile
    for kind in range(2):
        for zz in range(4):

            @pl.when(z != zz)
            def _():
                got(dist_ref.at[kind, zz], d_send.at[0, 0], d_recv.at[kind, zz])

    for when, make in placed:
        pl.when(when)(lambda: make().wait())
    for when, make in later:
        if when is None:
            make().wait_send()
        else:
            pl.when(when)(lambda: make().wait_send())


def layers_call(*arrays):
    vmem = pl.BlockSpec(memory_space=pltpu.VMEM)
    wide_a, wide_b = WIDE - UP0, UP0
    dma = pltpu.SemaphoreType.DMA
    return pl.pallas_call(
        layers_kernel,
        out_shape=(
            jax.ShapeDtypeStruct((SHARD, WIDE), f32),
            jax.ShapeDtypeStruct((SHARD, 128), f32),
            jax.ShapeDtypeStruct((2, 4, BLOCK, D), bf16),
        ),
        in_specs=[vmem] * 9 + [pl.BlockSpec(memory_space=pltpu.SMEM)] + [vmem],
        out_specs=(vmem, vmem, pl.BlockSpec(memory_space=pl.ANY)),
        scratch_shapes=[
            pltpu.VMEM((SHARD, WIDE), bf16),
            pltpu.VMEM((128, 128), f32),
            pltpu.VMEM((D, 640), bf16),
            pltpu.VMEM((2, 4, 2, 2, SHARD, WIDE), bf16),
            pltpu.VMEM((2, 4, 2, 2, SHARD, WIDE), bf16),
            pltpu.VMEM((ROWS, D), bf16),
            pltpu.VMEM((ROWS, D), bf16),
            pltpu.VMEM((ROWS, D), bf16),
            pltpu.VMEM((ROWS, D), bf16),
            pltpu.VMEM((ROWS, D), bf16),
            pltpu.VMEM((ROWS, D), bf16),
            pltpu.VMEM((D, 256), f32),
            pltpu.VMEM((2, ROWS, D), bf16),
            pltpu.VMEM((2, ROWS, D), bf16),
            pltpu.VMEM((2, ROWS, D), bf16),
            pltpu.VMEM((8, 3, QUARTER, D), bf16),
            pltpu.VMEM((8, ROWS, D), bf16),
            pltpu.VMEM((2, 8, ROWS, 384), bf16),
            pltpu.VMEM((2, ROWS, 256), bf16),
            pltpu.VMEM((2, ROWS, D), bf16),
            pltpu.VMEM((2, ROWS, D), f32),
            pltpu.VMEM((2, QUARTER, D), f32),
            pltpu.VMEM((2, 1, 3 * ROWS), f32),
            pltpu.VMEM((2, ROWS, 256), bf16),
            pltpu.VMEM((2, 16, D), f32),
            pltpu.VMEM((KEYS, 3 * ROWS), f32),
            pltpu.VMEM((256, 3 * ROWS), f32),
            pltpu.VMEM((2, 8, ROWS, 384), bf16),
            pltpu.VMEM((2, ROWS, 640), bf16),
            pltpu.VMEM((2, 4, ROWS, 384), bf16),
            pltpu.VMEM((2, 3, ROWS, 384), bf16),
            pltpu.VMEM((2, 128, D), f32),
            pltpu.VMEM((2, 4, 2, SHARD, wide_a), bf16),
            pltpu.VMEM((2, 4, 2, SHARD, wide_b), bf16),
            pltpu.VMEM((2, 4, 2, SHARD, wide_a), bf16),
            pltpu.VMEM((2, 4, 2, SHARD, wide_b), bf16),
            pltpu.VMEM((3, 4, SHARD, wide_a), bf16),
            pltpu.VMEM((3, 4, SHARD, wide_b), bf16),
            pltpu.VMEM((4, SHARD, wide_a), bf16),
            pltpu.VMEM((4, SHARD, wide_b), bf16),
            pltpu.VMEM((3, SHARD, wide_a), bf16),
            pltpu.VMEM((3, SHARD, wide_b), bf16),
            pltpu.VMEM((4, SHARD, 128), f32),
            dma((16, 3)), dma((16, 3)),
            dma((2, 7)), dma((2, 7)),
            dma((2, 7)), dma((2, 7)),
            dma((4, 7)), dma((4, 7)),
            dma((6, 7)), dma((6, 7)),
            dma((2,)), dma((2,)),
            dma((4, 2)), dma((2, 4)), dma((2,)),
            dma((3,)), dma((3,)),
        ],
        compiler_params=pltpu.CompilerParams(
            collective_id=0, has_side_effects=True, vmem_limit_bytes=VMEM_LIMIT
        ),
        name="layers",
    )(*arrays)


def on_device(
    frames, w_qkv, w_out, w_up, w_down, ln_gains, shifts, qv_bias, up_bias, lengths, out_grad
):
    own, tile, dist = layers_call(
        frames, jnp.transpose(w_qkv[0], (1, 0, 2)), w_out[0].T, w_up, w_down[0].T, ln_gains, shifts, qv_bias,
        up_bias, lengths, out_grad,
    )
    outs = dist.astype(f32)
    tile_t = tile.T
    little_t = own[:, OUT0 : OUT0 + 64].T
    grad_qkv = jnp.stack([own[:, 0:192], own[:, 256:448], own[:, 448:640]], axis=1)
    return (
        outs[0].reshape(1, 4, 1, BLOCK, D),
        outs[1].reshape(1, 4, 1, BLOCK, D),
        grad_qkv[None],
        own[:, OUT0 + 64 : UP0].T[None],
        own[:, UP0:DOWN0][None],
        own[:, DOWN0:WIDE].T[None],
        tile_t[0:2][None],
        tile_t[2:6][None],
        little_t[7:9, :12][None],
        little_t[6:7],
    )


def solution(mesh):
    in_specs = (
        P(None, None, "ctx", None),
        P("section", "ctx", None, "tp"),
        P("section", "tp", "ctx"),
        P("section", "ctx", "tp"),
        P("section", "tp", "ctx"),
        P("section", None, "ctx"),
        P("section", None, "ctx"),
        P("section", None, ("tp", "ctx")),
        P("section", ("tp", "ctx")),
        P(),
        P(None, None, "ctx", None),
    )
    out_specs = (
        P("section", None, None, "ctx", None),
        P("section", None, None, "ctx", None),
        P("section", "ctx", None, "tp"),
        P("section", "tp", "ctx"),
        P("section", "ctx", "tp"),
        P("section", "tp", "ctx"),
        P("section", None, "ctx"),
        P("section", None, "ctx"),
        P("section", None, ("tp", "ctx")),
        P("section", ("tp", "ctx")),
    )
    return jax.shard_map(
        on_device, mesh=mesh, in_specs=in_specs, out_specs=out_specs, check_vma=False
    )
```

```python
import functools

import jax
import jax.numpy as jnp
import numpy as np
from jax import lax
from jax.experimental import pallas as pl
from jax.experimental.pallas import tpu as pltpu
from jax.sharding import PartitionSpec as P

MESH = pl.DeviceIdType.MESH
f32 = jnp.float32
bf16 = jnp.bfloat16
epsilon = 1e-05
negative = -1e30

D = 768
SHARD = 48
QUARTER = 48
BLOCK = 96
ROWS = 192
KEYS = 1536
Q0, KV0, OUT0, UP0, DOWN0, WIDE = 0, 256, 640, 896, 1664, 2432
GROUPS = ((0, 48),)
VMEM_LIMIT = 60 * 1024 * 1024


def where_am_i():
    s = lax.axis_index("section")
    c = lax.axis_index("ctx")
    t = lax.axis_index("tp")
    y = lax.div(c, 4)
    zh = lax.rem(lax.div(c, 2), 2)
    core = lax.rem(c, 2)
    return y, zh * 2 + s, core, t


def ident(y, z, core, t):
    return {"section": lax.rem(z, 2), "ctx": y * 4 + lax.div(z, 2) * 2 + core, "tp": t}


def ring(i, d):
    return lax.rem(i + d, 4)


def greet(peers):
    barrier = pltpu.get_barrier_semaphore()
    for peer in peers:
        pl.semaphore_signal(barrier, inc=1, device_id=peer, device_id_type=MESH)
    pl.semaphore_wait(barrier, len(peers))


def remote(src, dst, send, recv, peer):
    return pltpu.make_async_remote_copy(
        src_ref=src, dst_ref=dst, send_sem=send, recv_sem=recv, device_id=peer, device_id_type=MESH
    )


def dot(a, b):
    return lax.dot_general(a, b, (((1,), (0,)), ((), ())), preferred_element_type=f32)


def dot_t(a, b):
    return lax.dot_general(a, b, (((1,), (1,)), ((), ())), preferred_element_type=f32)


def hat(v):
    center = v - jnp.mean(v, axis=-1, keepdims=True)
    r = lax.rsqrt(jnp.mean(center * center, axis=-1, keepdims=True) + epsilon)
    return center * r, r


def norm(v, gain, shift):
    return hat(v)[0] * gain + shift


def norm_back(v, gain, c):
    vhat, r = hat(v)
    cg = c * gain
    grad = r * (
        cg - jnp.mean(cg, axis=-1, keepdims=True) - vhat * jnp.mean(cg * vhat, axis=-1, keepdims=True)
    )
    return grad, jnp.sum(c * vhat, axis=0, keepdims=True), jnp.sum(c, axis=0, keepdims=True)


def layers_kernel(
    f_ref, wqkv_ref, wout_ref, wup_ref, wdown_ref, gains_ref, shifts_ref, qv_ref, up_ref, len_ref, og_ref,
    own_ref, small_ref, dist_ref,
    pack_ref, turned, sel_ref, w_ref, grads, x_all, g_all, x1_all, o1_all, gx1_all, gx0_all, both, gpre, gatt, gout, gmid, wo, att_all, m_all, n1, n2, ga, rs, part, kv, att, act, slope, mid, lse, q, small,
    scores, acc, dkv, dqkv, core_in, y_in, little,
    cin_a, cin_b, s_a, s_b, zin_a, zin_b, u_a, u_b, yin_a, yin_b, tiles,
    x_send, x_recv, k_send, k_recv, b_send, b_recv, w_send, w_recv, r_send, r_recv, f_send, f_recv,
    d_send, d_recv, d_local, t_send, t_recv, o_send, o_recv,
):
    y, z, core, t = where_am_i()
    other = 1 - core
    zh = lax.div(z, 2)
    mate = ident(y, z, other, t)

    def along_x(d):
        return ident(y, z, core, ring(t, d))

    def along_y(d):
        return ident(ring(y, d), z, core, t)

    def along_z(d):
        return ident(y, ring(z, d), core, t)

    greet(
        [along_x(d) for d in (1, 2, 3)]
        + [along_y(d) for d in (1, 2, 3)]
        + [along_z(d) for d in (1, 2, 3)]
        + [mate]
    )
    later = []


    turned[...] = jnp.zeros_like(turned)
    turned[0:2, 0:SHARD] = gains_ref[0].astype(f32)
    turned[2:6, 0:SHARD] = shifts_ref[0].astype(f32)
    turned[6:7, 0:SHARD] = up_ref[...].astype(f32)
    turned[7:9, 0:12] = qv_ref[0].astype(f32)
    pack_ref[:, OUT0:UP0] = jnp.concatenate(
        [turned[...].T[:SHARD, 0:64].astype(bf16), wout_ref[...]], axis=1
    )
    pack_ref[:, DOWN0:WIDE] = wdown_ref[...]
    pack_ref[:, UP0:DOWN0] = wup_ref[0]
    pack_ref[:, Q0:KV0] = jnp.concatenate([wqkv_ref[0], jnp.zeros((SHARD, 64), bf16)], axis=1)
    pack_ref[:, KV0:OUT0] = jnp.concatenate([wqkv_ref[1], wqkv_ref[2]], axis=1)

    def put(src, dst, send, recv, to, when=None):
        def make():
            return remote(src, dst, send, recv, to)

        if when is None:
            make().start()
        else:
            pl.when(when)(lambda: make().start())
        later.append((when, make))

    marks = [0, 0]

    def drain():
        n = marks.pop(0)
        for when, make in later[:n]:
            if when is None:
                make().wait_send()
            else:
                pl.when(when)(lambda make=make: make().wait_send())
        del later[:n]
        marks[:] = [m - n for m in marks] + [len(later)]

    def got(region, send, recv):
        remote(region, region, send, recv, mate).wait_recv()


    def cols(half):
        first, last = ((0, UP0), (UP0, DOWN0), (DOWN0, WIDE))[half]
        return pl.ds(first, last - first)

    first_core, second_core = core == 0, core == 1

    def holds(l):
        return lax.rem(z, 2) == l

    def lacks(l):
        return lax.rem(z, 2) != l

    def w_sems(l, half, i):
        return w_send.at[3 * l + half, i], w_recv.at[3 * l + half, i]

    def gather_a(l, half):
        here = w_ref.at[l, y, zh, core, :, cols(half)]
        src = pack_ref.at[:, cols(half)]
        for d in (1, 3, 2):
            put(src, here, *w_sems(l, half, d - 1), along_z(d), when=first_core & holds(l))
            put(src, here, *w_sems(l, half, d - 1), along_y(d), when=second_core & holds(l))

        @pl.when(holds(l))
        def _():
            w_ref[l, y, zh, core, :, cols(half)] = pack_ref[:, cols(half)]

    def from_z(d):
        return lax.div(ring(z, 4 - d), 2)

    def gather_b(l, half):
        c = cols(half)

        @pl.when(first_core & holds(l))
        def _():
            got(w_ref.at[l, y, from_z(2), core, :, c], *w_sems(l, half, 1))

        @pl.when(first_core & lacks(l))
        def _():
            for d in (1, 3):
                got(w_ref.at[l, y, from_z(d), core, :, c], *w_sems(l, half, d - 1))

        @pl.when(second_core & holds(l))
        def _():
            for d in (1, 3, 2):
                got(w_ref.at[l, ring(y, 4 - d), zh, core, :, c], *w_sems(l, half, d - 1))

        pair = w_ref.at[l, y, :, core, :, c]
        four = w_ref.at[l, :, zh, core, :, c]
        for d in (1, 3, 2):
            put(pair, pair, *w_sems(l, half, 2 + d), along_y(d), when=first_core)
            put(four, four, *w_sems(l, half, 2 + d), along_z(d), when=second_core & holds(l))

    def gather_c(l, half):
        c = cols(half)

        @pl.when(first_core)
        def _():
            for d in (1, 3, 2):
                got(w_ref.at[l, ring(y, 4 - d), :, core, :, c], *w_sems(l, half, 2 + d))

        @pl.when(second_core & holds(l))
        def _():
            got(w_ref.at[l, :, from_z(2), core, :, c], *w_sems(l, half, 4))

        @pl.when(second_core & lacks(l))
        def _():
            for d in (1, 3):
                got(w_ref.at[l, :, from_z(d), core, :, c], *w_sems(l, half, 2 + d))

        mine = w_ref.at[l, :, :, core, :, c]
        put(mine, mine, *w_sems(l, half, 6), mate)

    def gather_d(l, half):
        got(w_ref.at[l, :, :, other, :, cols(half)], *w_sems(l, half, 6))


    def out_sems(l, i):
        return o_send.at[l, i], o_recv.at[l, i]

    def fetch_out(l):
        src = w_ref.at[l, :, :, core, :, pl.ds(OUT0, UP0 - OUT0)]
        for d in (1, 3, 2):
            put(src, wo.at[l, t, :, :, core], *out_sems(l, d - 1), along_x(d))

    def pass_out(l):
        for d in (1, 3, 2):
            mine = wo.at[l, ring(t, 4 - d), :, :, core]
            got(mine, *out_sems(l, d - 1))
            put(mine, mine, *out_sems(l, 2 + d), mate)

    def have_out(l):
        for d in (1, 3, 2):
            got(wo.at[l, ring(t, 4 - d), :, :, other], *out_sems(l, 2 + d))

    def out_weight(l, i):
        return wo[l, i].reshape(D, UP0 - OUT0)

    def weight(l, first, last):
        return w_ref[l, :, :, :, :, first:last].reshape(D, last - first)


    pieces = {"ud": (UP0, WIDE, UP0, 1), "qkv": (Q0, OUT0, 0, 0), "out": (OUT0, UP0, 0, 0)}
    numbers = {"ud": 0, "qkv": 1, "out": 2}
    cin, s_out, zin, u_out, yin = (cin_b, cin_a), (s_b, s_a), (zin_b, zin_a), (u_b, u_a), (yin_b, yin_a)

    def r_sems(l, piece, i):
        return r_send.at[3 * l + numbers[piece], i], r_recv.at[3 * l + numbers[piece], i]

    def spans(piece):
        first, last, base, which = pieces[piece]
        return pl.ds(first, last - first), pl.ds(first - base, last - first), which

    def keep_grad(l, first, value):
        n = value.shape[1]
        grads[l, :, :, :, :, first : first + n] = value.astype(bf16).reshape(4, 2, 2, SHARD, n)

    def scatter_a(l, piece):
        wide, span, n = spans(piece)
        put(grads.at[l, :, :, other, :, wide], cin[n].at[l, :, :, :, span], *r_sems(l, piece, 0), mate)

    def scatter_b(l, piece):
        wide, span, n = spans(piece)
        got(cin[n].at[l, :, :, :, span], *r_sems(l, piece, 0))

        def add(i, carry):
            for b in range(2):
                s_out[n][l, i, b, :, span] = (
                    grads[l, i, b, core, :, wide].astype(f32) + cin[n][l, i, b, :, span].astype(f32)
                ).astype(bf16)
            return carry

        lax.fori_loop(0, 4, add, 0)
        for d in (2, 1, 3):
            put(s_out[n].at[l, :, lax.div(ring(z, d), 2), :, span], zin[n].at[d - 1, :, :, span],
                *r_sems(l, piece, d), along_z(d), when=holds(l) if d == 2 else lacks(l))

    def scatter_c(l, piece):
        wide, span, n = spans(piece)

        @pl.when(holds(l))
        def _():
            for d in (1, 3, 2):
                got(zin[n].at[d - 1, :, :, span], *r_sems(l, piece, d))

            def add(i, carry):
                total = s_out[n][l, i, zh, :, span].astype(f32)
                for d in (1, 2, 3):
                    total = total + zin[n][d - 1, i, :, span].astype(f32)
                u_out[n][i, :, span] = total.astype(bf16)
                return carry

            lax.fori_loop(0, 4, add, 0)

        for d in (2, 1, 3):
            put(u_out[n].at[ring(y, d), :, span], yin[n].at[d - 1, :, span], *r_sems(l, piece, 3 + d),
                along_y(d), when=holds(l))

    def scatter_d(l, piece):
        wide, span, n = spans(piece)

        @pl.when(holds(l))
        def _():
            total = u_out[n][y, :, span].astype(f32)
            for d in (1, 3, 2):
                got(yin[n].at[d - 1, :, span], *r_sems(l, piece, 3 + d))
                total = total + yin[n][d - 1, :, span].astype(f32)
            own_ref[:, wide] = total


    placed = []

    def place(l, kind, ref):
        for half in range(2):
            to_z = 2 * half + l
            src = ref.at[pl.ds(half * BLOCK, BLOCK)]
            dst = dist_ref.at[kind, z]
            put(src, dst, d_send.at[2 * l + kind, half], d_recv.at[kind, z], ident(y, to_z, core, t),
                when=z != to_z)
            make = functools.partial(pltpu.make_async_copy, src, dst, d_local.at[kind])
            start_here(z == to_z, make)
            placed.append((z == to_z, make))

    def start_here(when, make):
        pl.when(when)(lambda: make().start())


    def group(g):
        return slice(g[0], g[0] + 4 * g[1])

    def rows_of(g, i):
        return pl.ds(pl.multiple_of(g[0] + i * g[1], 16), g[1])

    def own_rows(g):
        return rows_of(g, t)

    def packed_rows(g):
        return slice(g[0] // 4, g[0] // 4 + g[1])

    def x_sems(phase, g, d):
        i = GROUPS.index(g) * 3 + d - 1
        return x_send.at[phase, i], x_recv.at[phase, i]

    def share_start(phase, ref, g):
        for d in (1, 3, 2):
            put(ref.at[own_rows(g)], ref.at[own_rows(g)], *x_sems(phase, g, d), along_x(d))

    def share_wait(phase, ref, g):
        for d in (1, 3, 2):
            got(ref.at[rows_of(g, ring(t, 4 - d))], *x_sems(phase, g, d))

    def sum_start(phase, i, g):
        at = pl.ds(g[0] // 4, g[1])
        for d in (1, 3, 2):
            put(part.at[i, rows_of(g, ring(t, d))], rs.at[i, d - 1, at], *x_sems(phase, g, d), along_x(d))

    def sum_wait(phase, i, g):
        total = part[i, own_rows(g), :].astype(f32)
        for d in (1, 3, 2):
            got(rs.at[i, d - 1, pl.ds(g[0] // 4, g[1])], *x_sems(phase, g, d))
            total = total + rs[i, d - 1, packed_rows(g), :].astype(f32)
        return total

    def share_all(phase, ref):
        for g in GROUPS:
            share_start(phase, ref, g)

    def shared_all(phase, ref):
        for g in GROUPS:
            share_wait(phase, ref, g)


    col = lax.broadcasted_iota(jnp.int32, (1, 256), 1)
    q_masks = [jnp.where((col >= 64 * i) & (col < 64 * i + 64), 1.0, 0.0).astype(f32) for i in range(3)]
    v_masks = [jnp.where((col >= 64 * i + 64) & (col < 64 * i + 128), 1.0, 0.0).astype(f32) for i in range(3)]

    def by_head(rows, masks):
        rows = rows.astype(f32)
        return jnp.concatenate([rows * m for m in masks], axis=0)

    def from_heads(rows, masks):
        return sum(rows[i * ROWS : (i + 1) * ROWS] * masks[i] for i in range(3))

    length = len_ref[0, z]
    within = lax.broadcasted_iota(jnp.int32, (ROWS, 1), 0)
    within = jnp.where(within >= BLOCK, within + BLOCK, within)

    def masked(b, s):
        first = (lax.div(b, 2) * 4 + lax.rem(b, 2)) * BLOCK
        return jnp.where(within < length - first, s, negative)

    def key_rows(b):
        return pl.ds(pl.multiple_of(b * ROWS, ROWS), ROWS)

    def k_sems(l, i):
        return k_send.at[l, i], k_recv.at[l, i]

    def key_part(l, b, g):
        return kv.at[l, b, pl.ds(g[0], 4 * g[1])]

    def send_keys(l, g):
        own = key_part(l, y * 2 + core, g)
        i = GROUPS.index(g)
        for d in (1, 3, 2):
            put(own, own, *k_sems(l, 3 * i + d - 1), along_y(d))
        put(own, own, *k_sems(l, 6 + i), mate)

    def attend(l, meanwhile):
        def sems(i):
            return k_send.at[l, i], k_recv.at[l, i]

        own = y * 2 + core
        q3 = by_head(q[l], q_masks).astype(bf16)

        def first(b, top):
            s = dot_t(kv[l, b, :, 0:256], q3)
            s = masked(b, s)
            scores[key_rows(b), :] = s
            return jnp.maximum(top, jnp.max(s, axis=0, keepdims=True))

        top = first(own, jnp.full((1, 3 * ROWS), negative, f32))
        for i, g in enumerate(GROUPS):
            got(key_part(l, y * 2 + other, g), *sems(6 + i))
        top = first(y * 2 + other, top)

        def same_core(i, top):
            d = 1 + 2 * i - 3 * lax.div(i, 2)
            b = ring(y, 4 - d) * 2 + core
            for j, g in enumerate(GROUPS):
                got(key_part(l, b, g), *sems(3 * j + d - 1))
            remote(kv.at[l, b], kv.at[l, b], *sems(7 + d), mate).start()
            return first(b, top)

        top = lax.fori_loop(0, 3, same_core, top)
        for d in (1, 2, 3):
            b = ring(y, 4 - d) * 2 + core
            later.append((None, functools.partial(remote, kv.at[l, b], kv.at[l, b], *sems(7 + d), mate)))

        def other_core(i, top):
            d = 1 + 2 * i - 3 * lax.div(i, 2)
            b = ring(y, 4 - d) * 2 + other
            got(kv.at[l, b], *sems(7 + d))
            return first(b, top)

        top = lax.fori_loop(0, 3, other_core, top)
        meanwhile()
        acc[...] = jnp.zeros_like(acc)

        def second(b, total):
            p = jnp.exp(scores[key_rows(b), :] - top)
            acc[...] += dot(kv[l, b, :, 128:384].T, p.astype(bf16))
            return total + jnp.sum(p, axis=0, keepdims=True)

        total = lax.fori_loop(0, 8, second, jnp.zeros((1, 3 * ROWS), f32))
        lse[l] = top + jnp.log(total)
        att[l] = from_heads((acc[...] / total).T, v_masks).astype(bf16)

    def prepare(l):
        q3 = by_head(q[l], q_masks).astype(bf16)
        log_total = lse[l]

        def step(b, carry):
            s = scores[key_rows(b), :] if l == 1 else masked(b, dot_t(kv[l, b, :, 0:256], q3))
            scores[key_rows(b), :] = jnp.exp(s - log_total)
            return carry

        lax.fori_loop(0, 8, step, 0)

    def attend_back(l, grad_att, meanwhile):
        def sems(i):
            return b_send.at[l, i], b_recv.at[l, i]

        q3 = by_head(q[l], q_masks).astype(bf16)
        do3 = by_head(grad_att, v_masks)
        delta = jnp.sum((do3 * by_head(att[l], v_masks)).T, axis=0, keepdims=True)
        do3 = do3.astype(bf16)
        acc[...] = jnp.zeros_like(acc)

        def block(b):
            k = kv[l, b, :, 0:256]
            p = scores[key_rows(b), :]
            ds = (p * (dot_t(kv[l, b, :, 128:384], do3) - delta)).astype(bf16)
            dk = dot(ds, q3)
            dv = dot(p.astype(bf16), do3)
            acc[...] += dot(k.T, ds)
            return jnp.concatenate([dk[:, :128], dk[:, 128:] + dv[:, :128], dv[:, 128:]], axis=1)

        def for_mate(off):
            b = ring(y, off) * 2 + other
            dkv[l, b] = block(b).astype(bf16)
            remote(dkv.at[l, b], core_in.at[l, off], *sems(off), mate).start()

        def step(i, carry):
            off = 2 + i - 3 * lax.div(i, 2)
            for_mate(off)
            b = ring(y, off) * 2 + core
            value = block(b)
            got(core_in.at[l, off], *sems(off))
            dkv[l, b] = (value + core_in[l, off].astype(f32)).astype(bf16)
            remote(dkv.at[l, b], y_in.at[l, off - 1], *sems(3 + off), along_y(off)).start()
            return carry

        lax.fori_loop(0, 3, step, 0)
        for_mate(0)
        for off in range(4):
            b = ring(y, off) * 2 + other
            later.append((None, functools.partial(remote, dkv.at[l, b], core_in.at[l, off], *sems(off), mate)))
        for off in (1, 2, 3):
            b = ring(y, off) * 2 + core
            later.append((None, functools.partial(
                remote, dkv.at[l, b], y_in.at[l, off - 1], *sems(3 + off), along_y(off))))
        total = block(y * 2 + core)
        dqkv[l, :, 0:256] = (from_heads(acc[...].T, q_masks) * 0.125).astype(bf16)
        got(core_in.at[l, 0], *sems(0))
        total = total + core_in[l, 0].astype(f32)
        meanwhile()
        for off in (1, 3, 2):
            got(y_in.at[l, off - 1], *sems(3 + off))
            total = total + y_in[l, off - 1].astype(f32)
        dqkv[l, :, 256:640] = total.astype(bf16)


    def load_small(l):
        small[l] = weight(l, OUT0, OUT0 + 128).astype(f32).T[:16]

    def forward(l, x_ref, x_phase, out_ref, out_phase, on_kv, on_sum, on_share, on_last):
        row = small[l]
        bias = dot(row.astype(bf16), sel_ref[...])
        for g in GROUPS:
            if x_phase is not None:
                share_wait(x_phase, x_ref, g)
            at = group(g)
            n1[l, at, :] = norm(x_ref[at, :].astype(f32), row[0:1], row[2:3]).astype(bf16)
            keys = dot(n1[l, at, :], weight(l, KV0, OUT0)) + bias[8:9, 256:]
            kv[l, y * 2 + core, at, :] = keys.astype(bf16)
            send_keys(l, g)
        if l == 1:
            fetch_out(l)
        queries = dot(n1[l], weight(l, Q0, KV0)) + bias[7:8, :256]
        q[l] = (queries.astype(bf16).astype(f32) * 0.125).astype(bf16)
        attend(l, on_kv)
        for d in (1, 3, 2):
            put(att.at[l], att_all.at[l, t], *x_sems(4 * l, GROUPS[0], d), along_x(d))
        m = x_ref[...].astype(f32) + dot_t(att[l], weight(l, OUT0, UP0)) + row[4:5]
        on_sum()
        drain()
        have_out(l)
        for d in (1, 3, 2):
            i = ring(t, 4 - d)
            got(att_all.at[l, i], *x_sems(4 * l, GROUPS[0], d))
            m = m + dot_t(att_all[l, i], out_weight(l, i))
        m_all[...] = m
        n2[l] = norm(m, row[1:2], row[3:4]).astype(bf16)
        on_share()
        for g in GROUPS:
            mid[l, packed_rows(g), :] = m_all[own_rows(g), :]
        kept = []
        for g in GROUPS:
            at = group(g)
            if g is GROUPS[0]:
                gather_d(l, 1)
            u = dot(n2[l, at, :], weight(l, UP0, DOWN0)) + row[6:7]
            phi = 0.5 * (1.0 + lax.erf(u * np.float32(0.5**0.5)))
            act[l, at, :] = (u * phi).astype(bf16)
            gather_d(l, 2)
            part[2 * l + 1, at, :] = dot_t(act[l, at, :], weight(l, DOWN0, WIDE)).astype(bf16)
            sum_start(4 * l + 2, 2 * l + 1, g)
            kept.append((at, u, phi))
        for at, u, phi in kept:
            slope[l, at, :] = phi + u * jnp.exp(-0.5 * u * u) * np.float32((2 * np.pi) ** -0.5)
        on_last()
        drain()
        for g in GROUPS:
            out = mid[l, packed_rows(g), :] + sum_wait(4 * l + 2, 2 * l + 1, g) + row[5:6]
            out_ref[own_rows(g), :] = out.astype(bf16)
            if out_phase is not None:
                share_start(out_phase, out_ref, g)

    def backward(l, d_ref, d_phase, x_ref, out_ref, out_phase, on_sum, on_share, on_att, on_last):
        base = 8 + 4 * (1 - l)
        row = small[l]
        little[l] = jnp.zeros_like(little[l])

        def note(i, value):
            little[l, i : i + 1, :] = little[l, i : i + 1, :] + jnp.sum(value, axis=0, keepdims=True)

        for g in GROUPS:
            at = group(g)
            if d_phase is not None:
                share_wait(d_phase, d_ref, g)
            gpre[at, :] = (dot(d_ref[at, :], weight(l, DOWN0, WIDE)) * slope[l, at, :]).astype(bf16)
            part[4 + 2 * l, at, :] = dot_t(gpre[at, :], weight(l, UP0, DOWN0)).astype(bf16)
            sum_start(base, 4 + 2 * l, g)
        keep_grad(l, UP0, dot(n2[l].T, gpre[...]))
        keep_grad(l, DOWN0, dot(d_ref[...].T, act[l]))
        note(6, gpre[...].astype(f32))
        on_sum()
        drain()
        for g in GROUPS:
            c = sum_wait(base, 4 + 2 * l, g)
            dout = d_ref[own_rows(g), :].astype(f32)
            gv, g_gain, g_shift = norm_back(mid[l, packed_rows(g), :], row[1:2], c)
            gm = dout + gv
            low = gm.astype(bf16)
            gmid[packed_rows(g), :] = gm
            ga[l, own_rows(g), :] = low
            for d in (2, 1, 3):
                gout[l, d - 1] = dot(low, out_weight(l, ring(t, d))).astype(bf16)
                put(gout.at[l, d - 1], gatt.at[l, own_rows(g)], *x_sems(4 * l + 1, g, d), along_x(d))
            gatt[l, own_rows(g), :] = dot(low, weight(l, OUT0, UP0)).astype(bf16)
            share_start(base + 1, ga.at[l], g)
            note(5, dout)
            note(1, g_gain)
            note(3, g_shift)
            note(4, low.astype(f32))
        prepare(l)
        on_share()
        drain()
        for g in GROUPS:
            for d in (1, 3, 2):
                got(gatt.at[l, rows_of(g, ring(t, 4 - d))], *x_sems(4 * l + 1, g, d))
        attend_back(l, gatt[l], on_att)
        for g in GROUPS:
            part[5 + 2 * l, group(g), :] = dot_t(dqkv[l, group(g), :], weight(l, Q0, OUT0)).astype(bf16)
            sum_start(base + 2, 5 + 2 * l, g)
        keep_grad(l, Q0, dot(n1[l].T, dqkv[l]))
        scatter_a(l, "qkv")
        sums = jnp.sum(dqkv[l].astype(f32), axis=0, keepdims=True)
        wide_col = lax.broadcasted_iota(jnp.int32, (8, 640), 1)
        which = lax.broadcasted_iota(jnp.int32, (8, 640), 0)
        two = jnp.where(((wide_col < 256) & (which == 0)) | ((wide_col >= 256) & (which == 1)), sums, 0.0)
        placed_rows = dot_t(two.astype(bf16), sel_ref[...])
        little[l, 7:9, :] = placed_rows[0:2]
        for g in GROUPS:
            share_wait(base + 1, ga.at[l], g)
        both[...] = dot(ga[l].T, att[l])
        on_last()
        drain()
        for g in GROUPS:
            c = sum_wait(base + 2, 5 + 2 * l, g)
            gv, g_gain, g_shift = norm_back(x_ref[own_rows(g), :].astype(f32), row[0:1], c)
            out_ref[own_rows(g), :] = (gmid[packed_rows(g), :] + gv).astype(bf16)
            share_start(out_phase, out_ref, g)
            note(0, g_gain)
            note(2, g_shift)

    def out_grads(l):
        keep_grad(l, OUT0, jnp.concatenate([both[:, :128] + little[l].T, both[:, 128:]], axis=1))


    B, U, V = 0, 1, 2
    gather_a(0, B)
    twin = ident(y, 3 - z, core, t)
    mine = pl.ds(pl.multiple_of(zh * BLOCK, BLOCK), BLOCK)
    theirs = pl.ds(pl.multiple_of((1 - zh) * BLOCK, BLOCK), BLOCK)
    put(f_ref.at[3 - z, 0], x_all.at[mine], f_send.at[0], f_recv.at[0], twin)
    row, column = (lax.broadcasted_iota(jnp.int32, (SHARD, 640), i) for i in range(2))
    for i in range(16):
        hit = ((column == row + 12 * i) | (column == row + 12 * i + 448)) & (row < 12)
        sel_ref[i * SHARD : (i + 1) * SHARD, :] = jnp.where(hit, 1.0, 0.0).astype(bf16)
    x_all[mine, :] = f_ref[z, 0]
    g_all[mine, :] = og_ref[z, 0]
    gather_b(0, B)
    gather_a(0, U)
    gather_a(0, V)
    put(og_ref.at[3 - z, 0], g_all.at[mine], f_send.at[1], f_recv.at[1], twin)
    gather_c(0, B)
    gather_b(0, U)
    fetch_out(0)
    got(x_all.at[theirs], f_send.at[0], f_recv.at[0])
    gather_d(0, B)
    load_small(0)

    def run(*steps):
        def body():
            for step in steps:
                step[0](*step[1:])

        return body

    forward(
        0, x_all, None, x1_all, 3,
        run((pass_out, 0), (gather_c, 0, U), (gather_b, 0, V)),
        run(),
        run((gather_c, 0, V), (gather_a, 1, B), (gather_a, 1, U), (gather_a, 1, V)),
        run((gather_b, 1, B), (gather_b, 1, U)),
    )
    gather_c(1, B)
    gather_d(1, B)
    load_small(1)
    forward(
        1, x1_all, 3, o1_all, None,
        run((pass_out, 1), (gather_c, 1, U), (gather_b, 1, V)), run(), run((gather_c, 1, V), (place, 0, 0, x1_all)),
        run(),
    )
    got(g_all.at[theirs], f_send.at[1], f_recv.at[1])
    backward(
        1, g_all, None, x1_all, gx1_all, 11,
        run((scatter_a, 1, "ud")), run((scatter_b, 1, "ud")), run((share_all, 7, o1_all)),
        run((scatter_c, 1, "ud")),
    )
    out_grads(1)
    scatter_a(1, "out")
    scatter_b(1, "qkv")
    backward(
        0, gx1_all, 11, x_all, gx0_all, 15,
        run((scatter_a, 0, "ud"), (scatter_b, 1, "out")),
        run((scatter_b, 0, "ud")),
        run((place, 1, 1, gx1_all), (shared_all, 7, o1_all), (place, 1, 0, o1_all)),
        run((scatter_c, 1, "qkv"), (scatter_c, 1, "out"), (scatter_c, 0, "ud"), (scatter_b, 0, "qkv")),
    )
    out_grads(0)
    scatter_a(0, "out")
    for piece in ("ud", "qkv", "out"):
        scatter_d(1, piece)
    scatter_c(0, "qkv")
    scatter_b(0, "out")
    scatter_d(0, "ud")
    shared_all(15, gx0_all)
    place(0, 1, gx0_all)
    scatter_c(0, "out")
    scatter_d(0, "qkv")
    scatter_d(0, "out")
    tiles[0] = own_ref[:, OUT0 : OUT0 + 128]
    for d in (1, 3, 2):
        put(tiles.at[0], tiles.at[d], t_send.at[d - 1], t_recv.at[d - 1], along_x(d))
    tile = tiles[0]
    for d in (1, 3, 2):
        got(tiles.at[d], t_send.at[d - 1], t_recv.at[d - 1])
        tile = tile + tiles[d]
    column = lax.broadcasted_iota(jnp.int32, (SHARD, 128), 1)
    turned[0:SHARD, :] = jnp.where(column < 6, tile, tiles[0])
    small_ref[...] = turned[...].T[:16]
    for kind in range(2):
        for zz in range(4):

            @pl.when(z != zz)
            def _():
                got(dist_ref.at[kind, zz], d_send.at[0, 0], d_recv.at[kind, zz])

    for when, make in placed:
        pl.when(when)(lambda: make().wait())
    for when, make in later:
        if when is None:
            make().wait_send()
        else:
            pl.when(when)(lambda: make().wait_send())


def layers_call(*arrays):
    vmem = pl.BlockSpec(memory_space=pltpu.VMEM)
    wide_a, wide_b = WIDE - UP0, UP0
    dma = pltpu.SemaphoreType.DMA
    return pl.pallas_call(
        layers_kernel,
        out_shape=(
            jax.ShapeDtypeStruct((SHARD, WIDE), f32),
            jax.ShapeDtypeStruct((16, 128), f32),
            jax.ShapeDtypeStruct((2, 4, BLOCK, D), bf16),
        ),
        in_specs=[vmem] * 9 + [pl.BlockSpec(memory_space=pltpu.SMEM)] + [vmem],
        out_specs=(vmem, vmem, pl.BlockSpec(memory_space=pl.ANY)),
        scratch_shapes=[
            pltpu.VMEM((SHARD, WIDE), bf16),
            pltpu.VMEM((128, 128), f32),
            pltpu.VMEM((D, 640), bf16),
            pltpu.VMEM((2, 4, 2, 2, SHARD, WIDE), bf16),
            pltpu.VMEM((2, 4, 2, 2, SHARD, WIDE), bf16),
            pltpu.VMEM((ROWS, D), bf16),
            pltpu.VMEM((ROWS, D), bf16),
            pltpu.VMEM((ROWS, D), bf16),
            pltpu.VMEM((ROWS, D), bf16),
            pltpu.VMEM((ROWS, D), bf16),
            pltpu.VMEM((ROWS, D), bf16),
            pltpu.VMEM((D, 256), f32),
            pltpu.VMEM((ROWS, D), bf16),
            pltpu.VMEM((2, ROWS, 256), bf16),
            pltpu.VMEM((2, 3, QUARTER, 256), bf16),
            pltpu.VMEM((QUARTER, D), f32),
            pltpu.VMEM((2, 4, 4, 2, 2, SHARD, UP0 - OUT0), bf16),
            pltpu.VMEM((2, 4, ROWS, 256), bf16),
            pltpu.VMEM((ROWS, D), f32),
            pltpu.VMEM((2, ROWS, D), bf16),
            pltpu.VMEM((2, ROWS, D), bf16),
            pltpu.VMEM((2, ROWS, D), bf16),
            pltpu.VMEM((8, 3, QUARTER, D), bf16),
            pltpu.VMEM((8, ROWS, D), bf16),
            pltpu.VMEM((2, 8, ROWS, 384), bf16),
            pltpu.VMEM((2, ROWS, 256), bf16),
            pltpu.VMEM((2, ROWS, D), bf16),
            pltpu.VMEM((2, ROWS, D), f32),
            pltpu.VMEM((2, QUARTER, D), f32),
            pltpu.VMEM((2, 1, 3 * ROWS), f32),
            pltpu.VMEM((2, ROWS, 256), bf16),
            pltpu.VMEM((2, 16, D), f32),
            pltpu.VMEM((KEYS, 3 * ROWS), f32),
            pltpu.VMEM((256, 3 * ROWS), f32),
            pltpu.VMEM((2, 8, ROWS, 384), bf16),
            pltpu.VMEM((2, ROWS, 640), bf16),
            pltpu.VMEM((2, 4, ROWS, 384), bf16),
            pltpu.VMEM((2, 3, ROWS, 384), bf16),
            pltpu.VMEM((2, 128, D), f32),
            pltpu.VMEM((2, 4, 2, SHARD, wide_a), bf16),
            pltpu.VMEM((2, 4, 2, SHARD, wide_b), bf16),
            pltpu.VMEM((2, 4, 2, SHARD, wide_a), bf16),
            pltpu.VMEM((2, 4, 2, SHARD, wide_b), bf16),
            pltpu.VMEM((3, 4, SHARD, wide_a), bf16),
            pltpu.VMEM((3, 4, SHARD, wide_b), bf16),
            pltpu.VMEM((4, SHARD, wide_a), bf16),
            pltpu.VMEM((4, SHARD, wide_b), bf16),
            pltpu.VMEM((3, SHARD, wide_a), bf16),
            pltpu.VMEM((3, SHARD, wide_b), bf16),
            pltpu.VMEM((4, SHARD, 128), f32),
            dma((16, 6)), dma((16, 6)),
            dma((2, 11)), dma((2, 11)),
            dma((2, 7)), dma((2, 7)),
            dma((6, 7)), dma((6, 7)),
            dma((6, 7)), dma((6, 7)),
            dma((2,)), dma((2,)),
            dma((4, 2)), dma((2, 4)), dma((2,)),
            dma((3,)), dma((3,)),
            dma((2, 6)), dma((2, 6)),
        ],
        compiler_params=pltpu.CompilerParams(
            collective_id=0, has_side_effects=True, vmem_limit_bytes=VMEM_LIMIT
        ),
        name="layers",
    )(*arrays)


def on_device(
    frames, w_qkv, w_out, w_up, w_down, ln_gains, shifts, qv_bias, up_bias, lengths, out_grad
):
    own, little, outputs = layers_call(
        frames, jnp.transpose(w_qkv[0], (1, 0, 2)), w_out[0].T, w_up, w_down[0].T, ln_gains, shifts, qv_bias,
        up_bias, lengths.T, out_grad,
    )
    outputs = outputs.astype(f32)
    grad_qkv = jnp.stack([own[:, 0:192], own[:, 256:448], own[:, 448:640]], axis=1)
    return (
        outputs[0].reshape(1, 4, 1, BLOCK, D),
        outputs[1].reshape(1, 4, 1, BLOCK, D),
        grad_qkv[None],
        own[:, OUT0 + 64 : UP0].T[None],
        own[:, UP0:DOWN0][None],
        own[:, DOWN0:WIDE].T[None],
        little[None, 0:2, :SHARD],
        little[None, 2:6, :SHARD],
        little[None, 7:9, :12],
        little[6:7, :SHARD],
    )


def solution(mesh):
    in_specs = (
        P(None, None, "ctx", None),
        P("section", "ctx", None, "tp"),
        P("section", "tp", "ctx"),
        P("section", "ctx", "tp"),
        P("section", "tp", "ctx"),
        P("section", None, "ctx"),
        P("section", None, "ctx"),
        P("section", None, ("tp", "ctx")),
        P("section", ("tp", "ctx")),
        P(),
        P(None, None, "ctx", None),
    )
    out_specs = (
        P("section", None, None, "ctx", None),
        P("section", None, None, "ctx", None),
        P("section", "ctx", None, "tp"),
        P("section", "tp", "ctx"),
        P("section", "ctx", "tp"),
        P("section", "tp", "ctx"),
        P("section", None, "ctx"),
        P("section", None, "ctx"),
        P("section", None, ("tp", "ctx")),
        P("section", ("tp", "ctx")),
    )
    return jax.shard_map(
        on_device, mesh=mesh, in_specs=in_specs, out_specs=out_specs, check_vma=False
    )
```
